512 devices in a mesh: chan: 8 (over x, core), filt: 16 (over z_lo, y), sp: 4 (over z_hi).
Axes of the slice: x: 4, y: 8, z: 8 (z_hi: 4, z_lo: 2; z = z_hi * 2 + z_lo), core: 2. Of those that a mesh axis runs over, the one named last changes fastest.
Arguments:
- activations: bfloat16 [512, 4, 2048], P('chan', 'sp', 'filt'), may hold values from -6 to 6
- weights: bfloat16 [3, 3, 3, 512, 512], P(None, None, None, 'chan', 'filt'), may hold values from -0.0546875 to 0.0546875
- out_grad: bfloat16 [512, 4, 2048], P('filt', 'sp', 'chan'), may hold values from -6 to 6
Outputs:
- responses: bfloat16 [512, 4, 2048], P('filt', 'sp', 'chan')
- in_grad: bfloat16 [512, 4, 2048], P('chan', 'sp', 'filt')
The draws below stay inside these ranges and needn't reach their ends.
All inputs are finite; a program needn't handle non-finite values.
Results may differ from the reference program's by a relative error of at most 0.001.
Values may be sent and summed in bfloat16 or wider, within the bound.
A program may use at most 64 MiB of HBM per device.

```python
import jax
import jax.numpy as jnp
from jax import lax

C = 512
F = 512
Y = 32
Z = 64
X = 4


def raised(entries, stream_key, source, target, parts, factor):
    owner, partner = [(jnp.arange(entries.shape[axis_at]) // (entries.shape[axis_at] // parts)).reshape([-1 if axis == axis_at else 1 for axis in range(entries.ndim)]) for axis_at in (source, target)]
    chosen = jax.random.permutation(stream_key, parts)[partner]
    strong = (owner == chosen) | (owner == (partner + parts // 2) % parts)
    return jnp.where(strong, factor * entries, entries)


def steps_of(rng, dims, split, least, largest):
    level = 1.0
    for dim, shards_of in split:
        draws = jax.random.uniform(jax.random.fold_in(jax.random.fold_in(rng, 6), dim), (shards_of,), jnp.float32, least / len(split), largest / len(split))
        level = level * jnp.repeat(jnp.exp(draws), dims[dim] // shards_of).reshape((-1,) + (1,) * (len(dims) - 1 - dim))
    return level


def normal_values(stream_key, extent, deviation, limit, cuts=(), dtype=jnp.bfloat16):
    array = jax.random.normal(stream_key, extent, jnp.float32) * deviation
    if len(cuts) > 0:
        array = steps_of(stream_key, extent, cuts, -0.22, 0.18) * array
    return jnp.clip(array, min=-limit, max=limit).astype(dtype)


def bell_draw_with(key, dims, width, reach, split, heavy, kind=jnp.bfloat16):
    result = width * jax.random.normal(key, dims, jnp.float32)
    if split:
        result = result * steps_of(key, dims, split, -0.22, 0.18)
    return jnp.clip(raised(result, jax.random.fold_in(key, 3), *heavy), -reach, reach).astype(kind)


def setup_inputs(seed: int = 0) -> dict:
    arg_keys = jax.random.split(jax.random.key(seed), 4)
    activations = bell_draw_with(arg_keys[0], (C, X, Y * Z), 1.0, 6.0, ((0, 8), (1, 4), (2, 16)), (0, 2, 16, 2.0))
    weights = normal_values(arg_keys[1], (3, 3, 3, C, F), (27 * C) ** -0.5, 0.0546875, ((3, 8), (4, 16)))
    out_grad = bell_draw_with(arg_keys[2], (F, X, Y * Z), 1.0, 6.0, ((0, 16), (1, 4), (2, 8)), (0, 2, 16, 2.0))
    return dict(activations=activations, weights=weights, out_grad=out_grad)


def convolve(volume, kernel, layout):
    return lax.conv_general_dilated(volume[None], kernel, (1, 1, 1), [(1, 1), (1, 1), (1, 1)], dimension_numbers=("NCDHW", layout, "NCDHW"), precision=lax.Precision.HIGHEST)[0]


def reference(activations, weights, out_grad):
    kernel = weights.astype(jnp.float32)
    volume = activations.astype(jnp.float32).reshape(C, X, Y, Z)
    cotangent = out_grad.astype(jnp.float32).reshape(F, X, Y, Z)
    responses = convolve(volume, kernel, "DHWIO")
    flipped = kernel[::-1, ::-1, ::-1]
    in_grad = convolve(cotangent, flipped, "DHWOI")
    return responses.reshape(F, X, Y * Z).astype(jnp.bfloat16), in_grad.reshape(C, X, Y * Z).astype(jnp.bfloat16)
```

```python
import functools

import jax
import jax.numpy as jnp
from jax import lax
from jax.experimental import pallas as pl
from jax.experimental.pallas import tpu as pltpu
from jax.sharding import PartitionSpec as P

MESH = pl.DeviceIdType.MESH
BF16 = jnp.bfloat16
F32 = jnp.float32
B = 32
LANES = 128


def kernel(
    nx, ny, ns,
    act_ref, w_hbm, og_ref, resp_ref, grad_ref,
    w_ref, d_ref, g_ref, hd_ref, hg_ref, wr_ref, lf_ref, lb_ref, r_ref,
    pb_ref, pf_ref, rb_ref, rf_ref,
    w_sem, loc_sem, f1_send, f1_recv, f2_send, f2_recv, b1_send, b1_recv, b2_send, b2_recv,
    ws_send, ws_recv, h_send, h_recv, b3_send, b3_recv, f3_send, f3_recv,
):
    xh = nx // 2
    tpb = ny // nx
    chan, filt, s = lax.axis_index("chan"), lax.axis_index("filt"), lax.axis_index("sp")
    x, core = chan // 2, chan % 2
    zl, y = filt // ny, filt % ny
    k, xi = x // xh, x % xh
    other = 1 - core
    first, last = s == 0, s == ns - 1
    inner = jnp.logical_and(s > 0, s < ns - 1)
    relay = core == k

    def dev(x_, core_, zl_, y_, s_):
        return (x_ * 2 + core_, zl_ * ny + y_, s_)

    def remote(src, dst, ssem, rsem, to):
        return pltpu.make_async_remote_copy(
            src_ref=src, dst_ref=dst, send_sem=ssem, recv_sem=rsem,
            device_id=to, device_id_type=MESH,
        )

    def on_slabs(body):
        pl.when(s > 0)(lambda: body(-1))
        pl.when(s < ns - 1)(lambda: body(1))
        body(0)

    load = pltpu.make_async_copy(w_hbm, w_ref, w_sem)
    load.start()

    barrier = pltpu.get_barrier_semaphore()

    def greet(to):
        pl.semaphore_signal(barrier, inc=1, device_id=to, device_id_type=MESH)

    def greet_slab(ds):
        for dc in range(2):
            for dz in range(2):
                if (ds, dc, dz) != (0, 0, 0):
                    greet(dev(x, (core + dc) % 2, (zl + dz) % 2, y, s + ds))

    on_slabs(greet_slab)
    for d in range(1, ny):
        greet(dev(x, core, zl, (y + d) % ny, s))
        for zs in range(2):
            greet(dev(x, zl, zs, (y + d) % ny, s))
    for d in range(1, nx):
        greet(dev((x + d) % nx, core, zl, y, s))

    def clear_planes(p):
        d_ref[y, p] = jnp.zeros(d_ref.shape[2:], BF16)

        @pl.when(relay)
        def _():
            for c in range(2):
                g_ref[xi, c, p] = jnp.zeros(g_ref.shape[3:], BF16)

    pl.when(first)(lambda: clear_planes(0))
    pl.when(last)(lambda: clear_planes(2))

    peers = 3 + 3 * (ny - 1) + (nx - 1)
    pl.semaphore_wait(barrier, peers + 8 - 4 * first.astype(jnp.int32) - 4 * last.astype(jnp.int32))

    def f1_copy(ds, dz):
        z2 = (zl + dz) % 2
        return (
            act_ref.at[pl.ds(z2 * B, B), :],
            d_ref.at[y, 1 - ds, pl.ds(core * B, B), :],
            f1_send.at[ds + 1, dz], f1_recv, dev(x, zl, z2, y, s + ds),
        )

    def b1_copy(ds, dz):
        z2 = (zl + dz) % 2
        return (
            og_ref,
            g_ref.at[xi, core, 1 - ds, pl.ds(zl * B, B), :],
            b1_send.at[ds + 1, dz], b1_recv, dev(x, k, z2, y, s + ds),
        )

    def start(args, own):
        if own is None:
            remote(*args).start()
            return
        pl.when(jnp.logical_not(own))(lambda: remote(*args).start())
        pl.when(own)(lambda: pltpu.make_async_copy(args[0], args[1], args[3]).start())

    def finish(args, own):
        if own is None:
            remote(*args).wait_send()
        else:
            pl.when(jnp.logical_not(own))(lambda: remote(*args).wait_send())

    def first_sends(act):
        def slab(ds):
            for dz in range(2):
                here = (ds, dz) == (0, 0)
                act(f1_copy(ds, dz), (core == zl) if here else None)
                act(b1_copy(ds, dz), relay if here else None)

        on_slabs(slab)

    first_sends(start)

    load.wait()
    blank = jnp.zeros((B, B), BF16)
    for a in range(3):
        for e in range(3):
            taps = [w_ref[a * 9 + b * 3 + e] for b in range(3)]
            for h in range(2):
                slot = jnp.where(zl == h, h, 2)
                fwd = jnp.concatenate([t[:, h * B:(h + 1) * B] for t in taps] + [blank], axis=1)
                flip = fwd.astype(F32).T
                bwd = jnp.concatenate([flip[(2 - b) * B:(3 - b) * B] for b in range(3)] + [flip[3 * B:]], axis=1)
                wr_ref[core, slot, 0, a * 3 + e] = fwd
                wr_ref[core, slot, 1, a * 3 + e] = bwd.astype(BF16)
    w_across = (wr_ref.at[core, 2], wr_ref.at[core, zl], ws_send.at[0], ws_recv.at[0], dev(x, core, 1 - zl, y, s))
    w_own = (wr_ref.at[core, zl], wr_ref.at[core, zl], ws_send.at[1], ws_recv.at[1], dev(x, other, zl, y, s))
    w_next = (wr_ref.at[core, 1 - zl], wr_ref.at[core, 1 - zl], ws_send.at[2], ws_recv.at[2], dev(x, other, zl, y, s))
    remote(*w_across).start()
    remote(*w_own).start()

    def wait_planes(whole, low, high, sem):
        pl.when(inner)(lambda: pltpu.make_async_copy(whole, whole, sem).wait())
        pl.when(first)(lambda: pltpu.make_async_copy(high, high, sem).wait())
        pl.when(last)(lambda: pltpu.make_async_copy(low, low, sem).wait())

    wait_planes_f1 = functools.partial(
        wait_planes, d_ref.at[y], d_ref.at[y, pl.ds(0, 2)], d_ref.at[y, pl.ds(1, 2)], f1_recv)

    def b2_copy(d):
        return (g_ref.at[xi], g_ref.at[xi], b2_send.at[d - 1], b2_recv.at[xi], dev((x + d) % nx, core, zl, y, s))

    def f2_copy(d):
        return (d_ref.at[y], d_ref.at[y], f2_send.at[d - 1], f2_recv.at[y], dev(x, core, zl, (y + d) % ny, s))

    wait_planes_f1()
    for d in range(1, ny):
        remote(*f2_copy(d)).start()

    @pl.when(relay)
    def _():
        wait_planes(g_ref.at[xi], g_ref.at[xi, :, pl.ds(0, 2)], g_ref.at[xi, :, pl.ds(1, 2)], b1_recv)
        for d in range(1, nx):
            remote(*b2_copy(d)).start()

    remote(*w_across).wait_recv()
    remote(*w_next).start()

    def halo_g(src_x, src_c, lane):
        return (g_ref.at[src_x, src_c, :, :, pl.ds(lane, LANES)], hg_ref, h_send.at[0], h_recv.at[0],
                dev(x, other, zl, y, s))

    def halo_d(src_y):
        return (d_ref.at[src_y], hd_ref, h_send.at[1], h_recv.at[1], dev(x, other, zl, y, s))

    for i in range(xh):
        @pl.when(jnp.logical_not(jnp.logical_and(relay, xi == i)))
        def _(i=i):
            pltpu.make_async_copy(g_ref.at[i], g_ref.at[i], b2_recv.at[i]).wait()

    low_g = halo_g(0, 0, 0)
    high_g = halo_g(xh - 1, 1, (tpb - 1) * LANES)
    pl.when(core == 0)(lambda: remote(*high_g).start())
    pl.when(core == 1)(lambda: remote(*low_g).start())

    remote(*w_own).wait_recv()
    remote(*w_next).wait_recv()
    for cs in range(2):
        for z in range(2):
            for a in range(3):
                for e in range(3):
                    lf_ref[e * 64 + z * B:e * 64 + z * B + B, a * 256 + cs * 128:a * 256 + cs * 128 + 128] = (
                        wr_ref[cs, z, 0, a * 3 + e])
                    lb_ref[e * 64 + cs * B:e * 64 + cs * B + B, a * 256 + z * 128:a * 256 + z * 128 + 128] = (
                        wr_ref[cs, z, 1, (2 - a) * 3 + 2 - e])
    for a in range(3):
        for c in range(2):
            row = a * 256 + c * 128 + 96
            r_ref[row:row + B, :] = jnp.zeros((B, r_ref.shape[1]), BF16)

    lane = lax.broadcasted_iota(jnp.int32, (64, LANES), 1)
    left_half = lane < 64
    inside_low = lane % 64 != 0
    inside_high = lane % 64 != 63

    def put(a, b, t, tile):
        for c in range(2):
            row = a * 256 + c * 128 + b * B
            r_ref[row:row + B, t * LANES:(t + 1) * LANES] = tile[c * B:(c + 1) * B]

    def rows(tile_of, halo_of):
        for a in range(3):
            halo = halo_of(a)
            none = jnp.zeros_like(halo)
            tiles = [jnp.where(core == 1, halo, none)]
            tiles += [tile_of(a, t) for t in range(ny)]
            tiles += [jnp.where(core == 0, halo, none)]
            turned = [pltpu.roll(t.astype(F32), 64, axis=1) for t in tiles]
            for t in range(ny + 1):
                mid = jnp.where(left_half, turned[t], turned[t + 1]).astype(BF16)
                if t < ny:
                    put(a, 0, t, mid)
                    put(a, 1, t, tiles[t + 1])
                if t > 0:
                    put(a, 2, t - 1, mid)

    def multiply(l_ref, emit):
        for pair in range(ny // 2):
            part = jnp.dot(l_ref[...], r_ref[:, pair * 256:(pair + 1) * 256], preferred_element_type=F32)
            for h in range(2):
                piece = part[:, h * LANES:(h + 1) * LANES]
                total = piece[64:128]
                total += jnp.where(inside_low, pltpu.roll(piece[0:64], 1, axis=1), 0.0)
                total += jnp.where(inside_high, pltpu.roll(piece[128:192], LANES - 1, axis=1), 0.0)
                emit(pair * 2 + h, total)

    pl.when(core == 0)(lambda: remote(*low_g).wait_recv())
    pl.when(core == 1)(lambda: remote(*high_g).wait_recv())

    def g_tile(a, t):
        j, h = t // tpb, t % tpb
        return g_ref[j // 2, j % 2, a, :, h * LANES:(h + 1) * LANES]

    rows(g_tile, lambda a: hg_ref[a])

    def emit_b(t, total):
        pb_ref[t] = total

    multiply(lb_ref, emit_b)

    def b3_copy(d, dc):
        y2, c2 = (y + d) % ny, (core + dc) % 2
        return (
            pb_ref.at[y2, pl.ds(c2 * B, B), :],
            rb_ref.at[y, pl.ds(zl * B, B), :],
            b3_send.at[d, dc], b3_recv, dev(x, c2, core, y2, s),
        )

    def b3_sends(act):
        for d in range(ny):
            for dc in range(2):
                act(b3_copy(d, dc), (core == zl) if (d, dc) == (0, 0) else None)

    b3_sends(start)

    for d in range(1, ny):
        y2 = (y + d) % ny
        pltpu.make_async_copy(d_ref.at[y2], d_ref.at[y2], f2_recv.at[y2]).wait()
    low_d = halo_d(0)
    high_d = halo_d(ny - 1)
    pl.when(core == 0)(lambda: remote(*high_d).start())
    pl.when(core == 1)(lambda: remote(*low_d).start())
    pl.when(core == 0)(lambda: remote(*low_d).wait_recv())
    pl.when(core == 1)(lambda: remote(*high_d).wait_recv())
    rows(lambda a, t: d_ref[t, a], lambda a: hd_ref[a])

    def emit_f(t, total):
        j, h = t // tpb, t % tpb
        for z in range(2):
            pf_ref[j, z, :, h * LANES:(h + 1) * LANES] = total[z * B:(z + 1) * B]

    multiply(lf_ref, emit_f)

    def f3_copy(j, dz):
        x2, c2, z2 = core * xh + j // 2, j % 2, (zl + dz) % 2
        return (
            pf_ref.at[j, z2], rf_ref.at[x, zl], f3_send.at[j, dz], f3_recv, dev(x2, c2, z2, y, s),
        ), jnp.logical_and(x2 == x, c2 == core)

    def f3_sends(act):
        for j in range(nx):
            for dz in range(2):
                copy, own = f3_copy(j, dz)
                act(copy, own if dz == 0 else None)

    f3_sends(start)

    pltpu.make_async_copy(rb_ref, rb_ref, b3_recv).wait()
    total = rb_ref[0]
    for i in range(1, ny):
        total += rb_ref[i]
    grad_ref[...] = total.astype(BF16)

    pltpu.make_async_copy(rf_ref, rf_ref, f3_recv).wait()
    total = rf_ref[0, 0]
    for i in range(1, nx * 2):
        total += rf_ref[i // 2, i % 2]
    resp_ref[...] = total.astype(BF16)

    first_sends(finish)
    for copy in (w_across, w_own, w_next):
        remote(*copy).wait_send()
    for d in range(1, ny):
        remote(*f2_copy(d)).wait_send()

    @pl.when(relay)
    def _():
        for d in range(1, nx):
            remote(*b2_copy(d)).wait_send()

    pl.when(core == 0)(lambda: remote(*high_g).wait_send())
    pl.when(core == 1)(lambda: remote(*low_g).wait_send())
    pl.when(core == 0)(lambda: remote(*high_d).wait_send())
    pl.when(core == 1)(lambda: remote(*low_d).wait_send())
    b3_sends(finish)
    f3_sends(finish)


def solution(mesh):
    nx, ny, ns = mesh.shape["chan"] // 2, mesh.shape["filt"] // 2, mesh.shape["sp"]
    xh = nx // 2

    def local(activations, weights, out_grad):
        act = activations.reshape(2 * B, LANES)
        grad = out_grad.reshape(B, -1)
        wide = grad.shape[1]
        w = jnp.swapaxes(weights, 3, 4).reshape(27, B, 2 * B)
        dma = pltpu.SemaphoreType.DMA
        responses, in_grad = pl.pallas_call(
            functools.partial(kernel, nx, ny, ns),
            out_shape=(
                jax.ShapeDtypeStruct((B, wide), BF16),
                jax.ShapeDtypeStruct((2 * B, LANES), BF16),
            ),
            in_specs=[
                pl.BlockSpec(memory_space=pltpu.VMEM),
                pl.BlockSpec(memory_space=pl.ANY),
                pl.BlockSpec(memory_space=pltpu.VMEM),
            ],
            out_specs=(pl.BlockSpec(memory_space=pltpu.VMEM),) * 2,
            scratch_shapes=[
                pltpu.VMEM((27, B, 2 * B), BF16),
                pltpu.VMEM((ny, 3, 2 * B, LANES), BF16),
                pltpu.VMEM((xh, 2, 3, 2 * B, wide), BF16),
                pltpu.VMEM((3, 2 * B, LANES), BF16),
                pltpu.VMEM((3, 2 * B, LANES), BF16),
                pltpu.VMEM((2, 3, 2, 9, B, LANES), BF16),
                pltpu.VMEM((192, 768), BF16),
                pltpu.VMEM((192, 768), BF16),
                pltpu.VMEM((768, ny * LANES), BF16),
                pltpu.VMEM((ny, 2 * B, LANES), F32),
                pltpu.VMEM((nx, 2, B, wide), F32),
                pltpu.VMEM((ny, 2 * B, LANES), F32),
                pltpu.VMEM((nx, 2, B, wide), F32),
                dma, dma,
                dma((3, 2)), dma,
                dma((ny - 1,)), dma((ny,)),
                dma((3, 2)), dma,
                dma((nx - 1,)), dma((xh,)),
                dma((3,)), dma((3,)),
                dma((2,)), dma((2,)),
                dma((ny, 2)), dma,
                dma((nx, 2)), dma,
            ],
            compiler_params=pltpu.CompilerParams(
                collective_id=0, has_side_effects=True, vmem_limit_bytes=32 * 1024 * 1024,
            ),
        )(act, w, grad)
        return responses.reshape(out_grad.shape), in_grad.reshape(activations.shape)

    return jax.shard_map(
        local,
        mesh=mesh,
        in_specs=(
            P("chan", "sp", "filt"),
            P(None, None, None, "chan", "filt"),
            P("filt", "sp", "chan"),
        ),
        out_specs=(P("filt", "sp", "chan"), P("chan", "sp", "filt")),
        check_vma=False,
    )
```

```python
import functools

import jax
import jax.numpy as jnp
from jax import lax
from jax.experimental import pallas as pl
from jax.experimental.pallas import tpu as pltpu
from jax.sharding import PartitionSpec as P

MESH = pl.DeviceIdType.MESH
BF16 = jnp.bfloat16
F32 = jnp.float32
B = 32
NX, NY = 4, 8
FAR = (4, 3, 5, 2, 6, 1, 7)
LANES = 128


def kernel(
    ns,
    act_hbm, w_hbm, og_hbm, resp_ref, grad_ref,
    a_ref, o_ref, w_ref, d_ref, g_ref, hd_ref, hg_ref, wr_ref, lf_ref, lb_ref, rg_ref, rd_ref,
    pb_ref, pf_ref, rb_ref, rf_ref,
    load_sem, f1_send, f1_recv, f2_send, f2_recv, b1_send, b1_recv, b2_send, b2_recv,
    ws_send, ws_recv, h_send, h_recv, b3_send, b3_recv, f3_send, f3_recv,
):
    chan, filt, s = lax.axis_index("chan"), lax.axis_index("filt"), lax.axis_index("sp")
    x, core = chan // 2, chan % 2
    zl, y = filt // NY, filt % NY
    k, xi = x // 2, x % 2
    other = 1 - core
    has_low, has_high = s > 0, s < ns - 1
    relay = core == k
    stays = core == zl

    def dev(x_, core_, zl_, y_, s_):
        return (x_ * 2 + core_, zl_ * NY + y_, s_)

    def remote(src, dst, ssem, rsem, to):
        return pltpu.make_async_remote_copy(
            src_ref=src, dst_ref=dst, send_sem=ssem, recv_sem=rsem,
            device_id=to, device_id_type=MESH,
        )

    def got(ref, sem):
        pltpu.make_async_copy(ref, ref, sem).wait()

    def start(args, own=None):
        if own is None:
            remote(*args).start()
            return
        pl.when(jnp.logical_not(own))(lambda: remote(*args).start())
        pl.when(own)(lambda: pltpu.make_async_copy(args[0], args[1], args[3]).start())

    def finish(args, own=None):
        if own is None:
            remote(*args).wait_send()
        else:
            pl.when(jnp.logical_not(own))(lambda: remote(*args).wait_send())

    barrier = pltpu.get_barrier_semaphore()

    def greet(to):
        pl.semaphore_signal(barrier, inc=1, device_id=to, device_id_type=MESH)

    loads = [
        pltpu.make_async_copy(act_hbm, a_ref.at[1], load_sem.at[0]),
        pltpu.make_async_copy(og_hbm, o_ref, load_sem.at[1]),
        pltpu.make_async_copy(w_hbm, w_ref, load_sem.at[2]),
    ]
    for load in loads:
        load.start()
    for d in FAR:
        for c in range(2):
            greet(dev(x, c, core, (y + d) % NY, s))

    def greet_slab(ds):
        for dc in range(2):
            for dz in range(2):
                if (ds, dc, dz) != (0, 0, 0):
                    greet(dev(x, (core + dc) % 2, (zl + dz) % 2, y, s + ds))

    pl.when(has_low)(lambda: greet_slab(-1))
    pl.when(has_high)(lambda: greet_slab(1))
    greet_slab(0)
    for d in range(1, NX):
        greet(dev((x + d) % NX, core, zl, y, s))

    def clear_planes(p):
        d_ref[:, p] = jnp.zeros((NY,) + d_ref.shape[2:], BF16)

        @pl.when(relay)
        def _():
            g_ref[xi, p] = jnp.zeros(g_ref.shape[2:], BF16)

    pl.when(jnp.logical_not(has_low))(lambda: clear_planes(0))
    pl.when(jnp.logical_not(has_high))(lambda: clear_planes(2))
    loads[0].wait()
    loads[1].wait()
    count = 2 * (NY - 1) + 3 + (NX - 1)
    pl.semaphore_wait(barrier, count + 4 * has_low.astype(jnp.int32) + 4 * has_high.astype(jnp.int32))

    def f1_copy(ds):
        return (a_ref.at[1], a_ref.at[1 - ds], f1_send.at[(ds + 1) // 2], f1_recv.at[(1 - ds) // 2],
                dev(x, core, zl, y, s + ds))

    def f2_sends(p):
        for d in (0,) + FAR:
            for dz in range(2):
                z2, y2 = (zl + dz) % 2, (y + d) % NY
                start((a_ref.at[p, pl.ds(z2 * B, B), :], d_ref.at[y, p, pl.ds(core * B, B), :],
                       f2_send.at[p], f2_recv.at[p], dev(x, zl, z2, y2, s)),
                      stays if (d, dz) == (0, 0) else None)

    def f2_finish(p):
        got(d_ref.at[pl.ds(0, NY - 1), p], f2_send.at[p])
        got(d_ref.at[NY - 1, p, pl.ds(0, B)], f2_send.at[p])
        pl.when(jnp.logical_not(stays))(lambda: got(d_ref.at[NY - 1, p, pl.ds(B, B)], f2_send.at[p]))

    def b1_copy(ds, dz):
        z2 = (zl + dz) % 2
        return (
            o_ref,
            g_ref.at[xi, 1 - ds, core, pl.ds(zl * B, B), :],
            b1_send.at[ds + 1, dz], b1_recv.at[1 - ds], dev(x, k, z2, y, s + ds),
        )

    def b1_sends(act):
        def slab(ds):
            for dz in range(2):
                act(b1_copy(ds, dz), relay if (ds, dz) == (0, 0) else None)

        pl.when(has_low)(lambda: slab(-1))
        pl.when(has_high)(lambda: slab(1))
        slab(0)

    pl.when(has_low)(lambda: start(f1_copy(-1)))
    pl.when(has_high)(lambda: start(f1_copy(1)))
    b1_sends(start)
    f2_sends(1)

    loads[2].wait()
    blank = jnp.zeros((B, B), BF16)
    for h in range(2):
        slot = jnp.where(zl == h, h, 2)
        for a in range(3):
            for e in range(3):
                taps = [w_ref[a * 9 + b * 3 + e] for b in range(3)]
                wr_ref[core, slot, 0, a * 3 + e] = jnp.concatenate(
                    [t[:, h * B:(h + 1) * B] for t in taps] + [blank], axis=1)
    w_across = (wr_ref.at[core, 2, 0], wr_ref.at[core, zl, 0], ws_send.at[0], ws_recv.at[0], dev(x, core, 1 - zl, y, s))
    w_own = (wr_ref.at[core, zl], wr_ref.at[core, zl], ws_send.at[1], ws_recv.at[1], dev(x, other, zl, y, s))
    w_next = (wr_ref.at[core, 1 - zl], wr_ref.at[core, 1 - zl], ws_send.at[2], ws_recv.at[2], dev(x, other, zl, y, s))
    start(w_across)

    def turn(slot):
        for i in range(9):
            flip = wr_ref[core, slot, 0, i].astype(F32).T
            wr_ref[core, slot, 1, i] = jnp.concatenate(
                [flip[(2 - b) * B:(3 - b) * B] for b in range(3)] + [flip[3 * B:]], axis=1).astype(BF16)

    def b2_copy(p, d):
        return (g_ref.at[xi, p], g_ref.at[xi, p], b2_send.at[p, d - 1], b2_recv.at[xi, p],
                dev((x + d) % NX, core, zl, y, s))

    def b2_sends(p):
        for d in (2, 1, 3):
            start(b2_copy(p, d))

    @pl.when(relay)
    def _():
        got(g_ref.at[xi, 1], b1_recv.at[1])
        b2_sends(1)

    @pl.when(has_low)
    def _():
        got(a_ref.at[0], f1_recv.at[0])
        f2_sends(0)

    @pl.when(has_high)
    def _():
        got(a_ref.at[2], f1_recv.at[1])
        f2_sends(2)

    @pl.when(relay)
    def _():
        pl.when(has_low)(lambda: got(g_ref.at[xi, 0], b1_recv.at[0]))
        b2_sends(0)
        pl.when(has_high)(lambda: got(g_ref.at[xi, 2], b1_recv.at[2]))
        b2_sends(2)

    turn(zl)
    start(w_own)
    got(wr_ref.at[core, 1 - zl, 0], ws_recv.at[0])
    turn(1 - zl)
    start(w_next)

    low_g = (g_ref.at[0, :, 0, :, pl.ds(0, LANES)], hg_ref, h_send.at[0], h_recv.at[0], dev(x, other, zl, y, s))
    high_g = (g_ref.at[1, :, 1, :, pl.ds(LANES, LANES)], hg_ref, h_send.at[0], h_recv.at[0], dev(x, other, zl, y, s))
    low_d = (d_ref.at[0], hd_ref, h_send.at[1], h_recv.at[1], dev(x, other, zl, y, s))
    high_d = (d_ref.at[NY - 1], hd_ref, h_send.at[1], h_recv.at[1], dev(x, other, zl, y, s))

    for i in range(2):
        @pl.when(jnp.logical_not(jnp.logical_and(relay, xi == i)))
        def _(i=i):
            for p in range(3):
                got(g_ref.at[i, p], b2_recv.at[i, p])

    pl.when(core == 0)(lambda: start(high_g))
    pl.when(core == 1)(lambda: start(low_g))

    remote(*w_own).wait_recv()
    remote(*w_next).wait_recv()
    for cs in range(2):
        for z in range(2):
            for a in range(3):
                for e in range(3):
                    lf_ref[e * 64 + z * B:e * 64 + z * B + B, a * 256 + cs * 128:a * 256 + cs * 128 + 128] = (
                        wr_ref[cs, z, 0, a * 3 + e])
                    lb_ref[e * 64 + cs * B:e * 64 + cs * B + B, a * 256 + z * 128:a * 256 + z * 128 + 128] = (
                        wr_ref[cs, z, 1, (2 - a) * 3 + 2 - e])

    lane = lax.broadcasted_iota(jnp.int32, (64, LANES), 1)
    left_half = lane < 64
    inside_low = lane % 64 != 0
    inside_high = lane % 64 != 63

    def put(r_ref, a, b, t, tile):
        for c in range(2):
            row = a * 256 + c * 128 + b * B
            r_ref[row:row + B, t * LANES:(t + 1) * LANES] = tile[c * B:(c + 1) * B]

    def half_turn(tile):
        return pltpu.roll(tile.astype(F32), 64, axis=1)

    def rows(r_ref, a, tile_of):
        for c in range(2):
            row = a * 256 + c * 128 + 3 * B
            r_ref[row:row + B, :] = jnp.zeros((B, r_ref.shape[1]), BF16)
        turned = None
        for t in range(NY):
            tile = tile_of(a, t)
            put(r_ref, a, 1, t, tile)
            before, turned = turned, half_turn(tile)
            if t > 0:
                mid = jnp.where(left_half, before, turned).astype(BF16)
                put(r_ref, a, 0, t, mid)
                put(r_ref, a, 2, t - 1, mid)

    def edge_rows(r_ref, a, tile_of, halo):
        turned = half_turn(halo)
        none = jnp.zeros_like(turned)
        low = jnp.where(core == 1, turned, none)
        high = jnp.where(core == 0, turned, none)
        put(r_ref, a, 0, 0, jnp.where(left_half, low, half_turn(tile_of(a, 0))).astype(BF16))
        put(r_ref, a, 2, NY - 1, jnp.where(left_half, half_turn(tile_of(a, NY - 1)), high).astype(BF16))

    def multiply(l_ref, r_ref, pair, emit):
        part = jnp.dot(l_ref[...], r_ref[:, pair * 256:(pair + 1) * 256], preferred_element_type=F32)
        for h in range(2):
            piece = part[:, h * LANES:(h + 1) * LANES]
            total = piece[64:128]
            total += jnp.where(inside_low, pltpu.roll(piece[0:64], 1, axis=1), 0.0)
            total += jnp.where(inside_high, pltpu.roll(piece[128:192], LANES - 1, axis=1), 0.0)
            emit(pair * 2 + h, total)

    def g_tile(a, t):
        return g_ref[t // 4, a, t // 2 % 2, :, t % 2 * LANES:(t % 2 + 1) * LANES]

    def emit_b(t, total):
        pb_ref[t] = total

    for a in range(3):
        rows(rg_ref, a, g_tile)
    for pair in (1, 2):
        multiply(lb_ref, rg_ref, pair, emit_b)
    pl.when(core == 0)(lambda: remote(*low_g).wait_recv())
    pl.when(core == 1)(lambda: remote(*high_g).wait_recv())
    for a in range(3):
        edge_rows(rg_ref, a, g_tile, hg_ref[a])
    for pair in (0, 3):
        multiply(lb_ref, rg_ref, pair, emit_b)

    got(d_ref.at[:, 1], f2_recv.at[1])
    for d in (0,) + FAR:
        for dc in range(2):
            y2, c2 = (y + d) % NY, (core + dc) % 2
            start((pb_ref.at[y2, pl.ds(c2 * B, B), :], rb_ref.at[y, pl.ds(zl * B, B), :],
                   b3_send, b3_recv, dev(x, c2, core, y2, s)),
                  stays if (d, dc) == (0, 0) else None)

    def d_tile(a, t):
        return d_ref[t, a]

    rows(rd_ref, 1, d_tile)
    pl.when(has_low)(lambda: got(d_ref.at[:, 0], f2_recv.at[0]))
    pl.when(has_high)(lambda: got(d_ref.at[:, 2], f2_recv.at[2]))
    pl.when(core == 0)(lambda: start(high_d))
    pl.when(core == 1)(lambda: start(low_d))
    rows(rd_ref, 0, d_tile)
    rows(rd_ref, 2, d_tile)

    def emit_f(t, total):
        for z in range(2):
            pf_ref[t // 2, z, :, t % 2 * LANES:(t % 2 + 1) * LANES] = total[z * B:(z + 1) * B]

    def f3_sends(j):
        for dz in range(2):
            x2, c2, z2 = core * 2 + j // 2, j % 2, (zl + dz) % 2
            own = jnp.logical_and(x2 == x, c2 == core) if dz == 0 else None
            start((pf_ref.at[j, z2], rf_ref.at[x, zl], f3_send.at[j, dz], f3_recv, dev(x2, c2, z2, y, s)), own)

    def f3_finish(j):
        for dz in range(2):
            x2, c2, z2 = core * 2 + j // 2, j % 2, (zl + dz) % 2
            own = jnp.logical_and(x2 == x, c2 == core) if dz == 0 else None
            finish((pf_ref.at[j, z2], rf_ref.at[x, zl], f3_send.at[j, dz], f3_recv, dev(x2, c2, z2, y, s)), own)

    for pair in (1, 2):
        multiply(lf_ref, rd_ref, pair, emit_f)
        f3_sends(pair)
    pl.when(core == 0)(lambda: remote(*low_d).wait_recv())
    pl.when(core == 1)(lambda: remote(*high_d).wait_recv())
    for a in range(3):
        edge_rows(rd_ref, a, d_tile, hd_ref[a])
    for pair in (0, 3):
        multiply(lf_ref, rd_ref, pair, emit_f)
        f3_sends(pair)

    got(rb_ref, b3_recv)
    total = rb_ref[0]
    for i in range(1, NY):
        total += rb_ref[i]
    grad_ref[...] = total.astype(BF16)

    pl.when(has_low)(lambda: finish(f1_copy(-1)))
    pl.when(has_high)(lambda: finish(f1_copy(1)))
    b1_sends(finish)
    f2_finish(1)
    pl.when(has_low)(lambda: f2_finish(0))
    pl.when(has_high)(lambda: f2_finish(2))
    for copy in (w_across, w_own, w_next):
        finish(copy)

    @pl.when(relay)
    def _():
        for p in range(3):
            for d in range(1, NX):
                finish(b2_copy(p, d))

    pl.when(core == 0)(lambda: finish(high_g))
    pl.when(core == 1)(lambda: finish(low_g))
    pl.when(core == 0)(lambda: finish(high_d))
    pl.when(core == 1)(lambda: finish(low_d))
    got(pb_ref.at[pl.ds(0, NY - 1)], b3_send)
    got(pb_ref.at[NY - 1, pl.ds(0, B)], b3_send)
    pl.when(jnp.logical_not(stays))(lambda: got(pb_ref.at[NY - 1, pl.ds(B, B)], b3_send))
    for j in range(NX):
        f3_finish(j)

    got(rf_ref, f3_recv)
    total = rf_ref[0, 0]
    for i in range(1, NX * 2):
        total += rf_ref[i // 2, i % 2]
    resp_ref[...] = total.astype(BF16)


def solution(mesh):
    ns = mesh.shape["sp"]

    def local(activations, weights, out_grad):
        act = activations.reshape(2 * B, LANES)
        grad = out_grad.reshape(B, -1)
        wide = grad.shape[1]
        w = jnp.swapaxes(weights, 3, 4).reshape(27, B, 2 * B)
        dma = pltpu.SemaphoreType.DMA
        responses, in_grad = pl.pallas_call(
            functools.partial(kernel, ns),
            out_shape=(
                jax.ShapeDtypeStruct((B, wide), BF16),
                jax.ShapeDtypeStruct((2 * B, LANES), BF16),
            ),
            in_specs=[pl.BlockSpec(memory_space=pl.ANY)] * 3,
            out_specs=(pl.BlockSpec(memory_space=pltpu.VMEM),) * 2,
            scratch_shapes=[
                pltpu.VMEM((3, 2 * B, LANES), BF16),
                pltpu.VMEM((B, wide), BF16),
                pltpu.VMEM((27, B, 2 * B), BF16),
                pltpu.VMEM((NY, 3, 2 * B, LANES), BF16),
                pltpu.VMEM((2, 3, 2, 2 * B, wide), BF16),
                pltpu.VMEM((3, 2 * B, LANES), BF16),
                pltpu.VMEM((3, 2 * B, LANES), BF16),
                pltpu.VMEM((2, 3, 2, 9, B, LANES), BF16),
                pltpu.VMEM((192, 768), BF16),
                pltpu.VMEM((192, 768), BF16),
                pltpu.VMEM((768, NY * LANES), BF16),
                pltpu.VMEM((768, NY * LANES), BF16),
                pltpu.VMEM((NY, 2 * B, LANES), F32),
                pltpu.VMEM((NX, 2, B, wide), F32),
                pltpu.VMEM((NY, 2 * B, LANES), F32),
                pltpu.VMEM((NX, 2, B, wide), F32),
                dma((3,)),
                dma((2,)), dma((2,)),
                dma((3,)), dma((3,)),
                dma((3, 2)), dma((3,)),
                dma((3, NX - 1)), dma((2, 3)),
                dma((3,)), dma((3,)),
                dma((2,)), dma((2,)),
                dma, dma,
                dma((NX, 2)), dma,
            ],
            compiler_params=pltpu.CompilerParams(
                collective_id=0, has_side_effects=True, vmem_limit_bytes=60 * 1024 * 1024,
            ),
        )(act, w, grad)
        return responses.reshape(out_grad.shape), in_grad.reshape(activations.shape)

    return jax.shard_map(
        local,
        mesh=mesh,
        in_specs=(
            P("chan", "sp", "filt"),
            P(None, None, None, "chan", "filt"),
            P("filt", "sp", "chan"),
        ),
        out_specs=(P("filt", "sp", "chan"), P("chan", "sp", "filt")),
        check_vma=False,
    )
```

```python
import functools

import jax
import jax.numpy as jnp
from jax import lax
from jax.experimental import pallas as pl
from jax.experimental.pallas import tpu as pltpu
from jax.sharding import PartitionSpec as P

MESH = pl.DeviceIdType.MESH
BF16 = jnp.bfloat16
F32 = jnp.float32
B = 32
NX, NY = 4, 8
FAR = (4, 3, 5, 2, 6, 1, 7)
LANES = 128


def kernel(
    ns,
    act_hbm, w_hbm, og_hbm, resp_ref, grad_ref,
    a_ref, o_ref, w_ref, d_ref, g_ref, hd_ref, hg_ref, wr_ref, lf_ref, lb_ref, rg_ref, rd_ref,
    pb_ref, pf_ref, rb_ref, rf_ref,
    load_sem, f1_send, f1_recv, f2_send, f2_recv, b1_send, b1_recv, b2_send, b2_recv,
    ws_send, ws_recv, h_send, h_recv, b3_send, b3_recv, f3_send, f3_recv,
):
    chan, filt, s = lax.axis_index("chan"), lax.axis_index("filt"), lax.axis_index("sp")
    x, core = chan // 2, chan % 2
    zl, y = filt // NY, filt % NY
    k, xi = x // 2, x % 2
    other = 1 - core
    has_low, has_high = s > 0, s < ns - 1
    relay = core == k
    stays = core == zl

    def dev(x_, core_, zl_, y_, s_):
        return (x_ * 2 + core_, zl_ * NY + y_, s_)

    def remote(src, dst, ssem, rsem, to):
        return pltpu.make_async_remote_copy(
            src_ref=src, dst_ref=dst, send_sem=ssem, recv_sem=rsem,
            device_id=to, device_id_type=MESH,
        )

    def got(ref, sem):
        pltpu.make_async_copy(ref, ref, sem).wait()

    def start(args, own=None):
        if own is None:
            remote(*args).start()
            return
        pl.when(jnp.logical_not(own))(lambda: remote(*args).start())
        pl.when(own)(lambda: pltpu.make_async_copy(args[0], args[1], args[3]).start())

    def finish(args, own=None):
        if own is None:
            remote(*args).wait_send()
        else:
            pl.when(jnp.logical_not(own))(lambda: remote(*args).wait_send())

    barrier = pltpu.get_barrier_semaphore()

    def greet(to):
        pl.semaphore_signal(barrier, inc=1, device_id=to, device_id_type=MESH)

    loads = [
        pltpu.make_async_copy(act_hbm, a_ref.at[1], load_sem.at[0]),
        pltpu.make_async_copy(og_hbm, o_ref, load_sem.at[1]),
        pltpu.make_async_copy(w_hbm, w_ref, load_sem.at[2]),
    ]
    for load in loads:
        load.start()
    for d in FAR:
        for c in range(2):
            greet(dev(x, c, core, (y + d) % NY, s))

    def greet_slab(ds):
        for dc in range(2):
            for dz in range(2):
                if (ds, dc, dz) != (0, 0, 0):
                    greet(dev(x, (core + dc) % 2, (zl + dz) % 2, y, s + ds))

    pl.when(has_low)(lambda: greet_slab(-1))
    pl.when(has_high)(lambda: greet_slab(1))
    greet_slab(0)
    for d in range(1, NX):
        greet(dev((x + d) % NX, core, zl, y, s))

    def clear_planes(p):
        d_ref[:, p] = jnp.zeros((NY,) + d_ref.shape[2:], BF16)

        @pl.when(relay)
        def _():
            g_ref[xi, p] = jnp.zeros(g_ref.shape[2:], BF16)

    pl.when(jnp.logical_not(has_low))(lambda: clear_planes(0))
    pl.when(jnp.logical_not(has_high))(lambda: clear_planes(2))
    loads[0].wait()
    loads[1].wait()
    count = 2 * (NY - 1) + 3 + (NX - 1)
    pl.semaphore_wait(barrier, count + 4 * has_low.astype(jnp.int32) + 4 * has_high.astype(jnp.int32))

    def f1_copy(ds):
        return (a_ref.at[1], a_ref.at[1 - ds], f1_send.at[(ds + 1) // 2], f1_recv.at[(1 - ds) // 2],
                dev(x, core, zl, y, s + ds))

    def f2_sends(p, across):
        for d in (0,) + FAR:
            for dz in across:
                z2, y2 = (zl + dz) % 2, (y + d) % NY
                start((a_ref.at[p, pl.ds(z2 * B, B), :], d_ref.at[y, p, pl.ds(core * B, B), :],
                       f2_send.at[p], f2_recv.at[p], dev(x, zl, z2, y2, s)),
                      stays if (d, dz) == (0, 0) else None)

    def f2_finish(p):
        got(d_ref.at[pl.ds(0, NY - 1), p], f2_send.at[p])
        got(d_ref.at[NY - 1, p, pl.ds(0, B)], f2_send.at[p])
        pl.when(jnp.logical_not(stays))(lambda: got(d_ref.at[NY - 1, p, pl.ds(B, B)], f2_send.at[p]))

    def b1_copy(ds, dz):
        z2 = (zl + dz) % 2
        return (
            o_ref,
            g_ref.at[xi, 1 - ds, core, pl.ds(zl * B, B), :],
            b1_send.at[ds + 1], b1_recv.at[1 - ds], dev(x, k, z2, y, s + ds),
        )

    def b1_sends(ds):
        for dz in range(2):
            start(b1_copy(ds, dz), relay if (ds, dz) == (0, 0) else None)

    pl.when(has_low)(lambda: start(f1_copy(-1)))
    pl.when(has_high)(lambda: start(f1_copy(1)))
    pl.when(has_low)(lambda: b1_sends(-1))
    pl.when(has_high)(lambda: b1_sends(1))
    b1_sends(0)
    f2_sends(1, (0,))

    loads[2].wait()
    blank = jnp.zeros((B, B), BF16)
    for h in range(2):
        slot = jnp.where(zl == h, h, 2)
        for a in range(3):
            for e in range(3):
                taps = [w_ref[a * 9 + b * 3 + e] for b in range(3)]
                wr_ref[core, slot, 0, a * 3 + e] = jnp.concatenate(
                    [t[:, h * B:(h + 1) * B] for t in taps] + [blank], axis=1)
    w_across = (wr_ref.at[core, 2, 0], wr_ref.at[core, zl, 0], ws_send.at[0], ws_recv.at[0], dev(x, core, 1 - zl, y, s))
    w_own = (wr_ref.at[core, zl], wr_ref.at[core, zl], ws_send.at[1], ws_recv.at[1], dev(x, other, zl, y, s))
    w_next = (wr_ref.at[core, 1 - zl], wr_ref.at[core, 1 - zl], ws_send.at[2], ws_recv.at[2], dev(x, other, zl, y, s))
    start(w_across)

    def turn(slot):
        for i in range(9):
            flip = wr_ref[core, slot, 0, i].astype(F32).T
            wr_ref[core, slot, 1, i] = jnp.concatenate(
                [flip[(2 - b) * B:(3 - b) * B] for b in range(3)] + [flip[3 * B:]], axis=1).astype(BF16)

    def b2_copy(p, d):
        return (g_ref.at[xi, p], g_ref.at[xi, p], b2_send.at[p], b2_recv.at[xi, p],
                dev((x + d) % NX, core, zl, y, s))

    def b2_sends(p):
        for d in (2, 1, 3):
            start(b2_copy(p, d))

    @pl.when(relay)
    def _():
        got(g_ref.at[xi, 1], b1_recv.at[1])
        b2_sends(1)

    f2_sends(1, (1,))

    @pl.when(has_low)
    def _():
        got(a_ref.at[0], f1_recv.at[0])
        f2_sends(0, (0, 1))

    @pl.when(has_high)
    def _():
        got(a_ref.at[2], f1_recv.at[1])
        f2_sends(2, (0, 1))

    @pl.when(relay)
    def _():
        pl.when(has_low)(lambda: got(g_ref.at[xi, 0], b1_recv.at[0]))
        b2_sends(0)
        pl.when(has_high)(lambda: got(g_ref.at[xi, 2], b1_recv.at[2]))
        b2_sends(2)

    turn(zl)
    start(w_own)
    got(wr_ref.at[core, 1 - zl, 0], ws_recv.at[0])
    turn(1 - zl)
    start(w_next)

    low_g = (g_ref.at[0, :, 0, :, pl.ds(0, LANES)], hg_ref, h_send.at[0], h_recv.at[0], dev(x, other, zl, y, s))
    high_g = (g_ref.at[1, :, 1, :, pl.ds(LANES, LANES)], hg_ref, h_send.at[0], h_recv.at[0], dev(x, other, zl, y, s))
    low_d = (d_ref.at[0], hd_ref, h_send.at[1], h_recv.at[1], dev(x, other, zl, y, s))
    high_d = (d_ref.at[NY - 1], hd_ref, h_send.at[1], h_recv.at[1], dev(x, other, zl, y, s))

    for i in range(2):
        @pl.when(jnp.logical_not(jnp.logical_and(relay, xi == i)))
        def _(i=i):
            for p in range(3):
                got(g_ref.at[i, p], b2_recv.at[i, p])

    pl.when(core == 0)(lambda: start(high_g))
    pl.when(core == 1)(lambda: start(low_g))

    remote(*w_own).wait_recv()
    remote(*w_next).wait_recv()
    for cs in range(2):
        for z in range(2):
            for a in range(3):
                for e in range(3):
                    lf_ref[e * 64 + z * B:e * 64 + z * B + B, a * 256 + cs * 128:a * 256 + cs * 128 + 128] = (
                        wr_ref[cs, z, 0, a * 3 + e])
                    lb_ref[e * 64 + cs * B:e * 64 + cs * B + B, a * 256 + z * 128:a * 256 + z * 128 + 128] = (
                        wr_ref[cs, z, 1, (2 - a) * 3 + 2 - e])

    lane = lax.broadcasted_iota(jnp.int32, (64, LANES), 1)
    left_half = lane < 64
    inside_low = lane % 64 != 0
    inside_high = lane % 64 != 63

    def put(r_ref, a, b, t, tile):
        for c in range(2):
            row = a * 256 + c * 128 + b * B
            r_ref[row:row + B, t * LANES:(t + 1) * LANES] = tile[c * B:(c + 1) * B]

    def half_turn(tile):
        return pltpu.roll(tile.astype(F32), 64, axis=1)

    def rows(r_ref, a, tile_of):
        for c in range(2):
            row = a * 256 + c * 128 + 3 * B
            r_ref[row:row + B, :] = jnp.zeros((B, r_ref.shape[1]), BF16)
        turned = None
        for t in range(NY):
            tile = tile_of(a, t)
            put(r_ref, a, 1, t, tile)
            before, turned = turned, half_turn(tile)
            if t > 0:
                mid = jnp.where(left_half, before, turned).astype(BF16)
                put(r_ref, a, 0, t, mid)
                put(r_ref, a, 2, t - 1, mid)

    def edge_rows(r_ref, a, tile_of, halo):
        turned = half_turn(halo)
        none = jnp.zeros_like(turned)
        low = jnp.where(core == 1, turned, none)
        high = jnp.where(core == 0, turned, none)
        put(r_ref, a, 0, 0, jnp.where(left_half, low, half_turn(tile_of(a, 0))).astype(BF16))
        put(r_ref, a, 2, NY - 1, jnp.where(left_half, half_turn(tile_of(a, NY - 1)), high).astype(BF16))

    def multiply(l_ref, r_ref, pair, emit):
        part = jnp.dot(l_ref[...], r_ref[:, pair * 256:(pair + 1) * 256], preferred_element_type=F32)
        for h in range(2):
            piece = part[:, h * LANES:(h + 1) * LANES]
            total = piece[64:128]
            total += jnp.where(inside_low, pltpu.roll(piece[0:64], 1, axis=1), 0.0)
            total += jnp.where(inside_high, pltpu.roll(piece[128:192], LANES - 1, axis=1), 0.0)
            emit(pair * 2 + h, total)

    def g_tile(a, t):
        return g_ref[t // 4, a, t // 2 % 2, :, t % 2 * LANES:(t % 2 + 1) * LANES]

    def emit_b(t, total):
        pb_ref[t] = total

    def b3_sends(tiles):
        for t in tiles:
            for dc in range(2):
                c2 = (core + dc) % 2
                start((pb_ref.at[t, pl.ds(c2 * B, B), :], rb_ref.at[y, pl.ds(zl * B, B), :],
                       b3_send, b3_recv, dev(x, c2, core, t, s)),
                      jnp.logical_and(stays, y == t) if dc == 0 else None)

    for a in range(3):
        rows(rg_ref, a, g_tile)
    for pair in (1, 2):
        multiply(lb_ref, rg_ref, pair, emit_b)
    got(d_ref.at[:, 1], f2_recv.at[1])
    b3_sends((4, 3, 5, 2))
    pl.when(core == 0)(lambda: remote(*low_g).wait_recv())
    pl.when(core == 1)(lambda: remote(*high_g).wait_recv())
    for a in range(3):
        edge_rows(rg_ref, a, g_tile, hg_ref[a])
    for pair in (0, 3):
        multiply(lb_ref, rg_ref, pair, emit_b)
    b3_sends((0, 7, 1, 6))

    def d_tile(a, t):
        return d_ref[t, a]

    rows(rd_ref, 1, d_tile)
    pl.when(has_low)(lambda: got(d_ref.at[:, 0], f2_recv.at[0]))
    pl.when(has_high)(lambda: got(d_ref.at[:, 2], f2_recv.at[2]))
    pl.when(core == 0)(lambda: start(high_d))
    pl.when(core == 1)(lambda: start(low_d))
    rows(rd_ref, 0, d_tile)
    rows(rd_ref, 2, d_tile)

    def emit_f(t, total):
        for z in range(2):
            pf_ref[t // 2, z, :, t % 2 * LANES:(t % 2 + 1) * LANES] = total[z * B:(z + 1) * B]

    def f3_sends(j):
        for dz in range(2):
            x2, c2, z2 = core * 2 + j // 2, j % 2, (zl + dz) % 2
            own = jnp.logical_and(x2 == x, c2 == core) if dz == 0 else None
            start((pf_ref.at[j, z2], rf_ref.at[x, zl], f3_send, f3_recv, dev(x2, c2, z2, y, s)), own)

    for pair in (1, 2):
        multiply(lf_ref, rd_ref, pair, emit_f)
        f3_sends(pair)
    pl.when(core == 0)(lambda: remote(*low_d).wait_recv())
    pl.when(core == 1)(lambda: remote(*high_d).wait_recv())
    for a in range(3):
        edge_rows(rd_ref, a, d_tile, hd_ref[a])
    for pair in (0, 3):
        multiply(lf_ref, rd_ref, pair, emit_f)
        f3_sends(pair)

    pl.when(has_low)(lambda: finish(f1_copy(-1)))
    pl.when(has_high)(lambda: finish(f1_copy(1)))
    pair = g_ref.at[0, 0, 0]
    pl.when(has_low)(lambda: got(pair, b1_send.at[0]))
    pl.when(has_high)(lambda: got(pair, b1_send.at[2]))
    pl.when(relay)(lambda: got(pair.at[pl.ds(0, B)], b1_send.at[1]))
    pl.when(jnp.logical_not(relay))(lambda: got(pair, b1_send.at[1]))
    f2_finish(1)
    pl.when(has_low)(lambda: f2_finish(0))
    pl.when(has_high)(lambda: f2_finish(2))
    for copy in (w_across, w_own, w_next):
        finish(copy)

    @pl.when(relay)
    def _():
        for p in range(3):
            got(g_ref.at[0], b2_send.at[p])

    pl.when(core == 0)(lambda: finish(high_g))
    pl.when(core == 1)(lambda: finish(low_g))
    pl.when(core == 0)(lambda: finish(high_d))
    pl.when(core == 1)(lambda: finish(low_d))
    got(pb_ref.at[pl.ds(0, NY - 1)], b3_send)
    got(pb_ref.at[NY - 1, pl.ds(0, B)], b3_send)
    pl.when(jnp.logical_not(stays))(lambda: got(pb_ref.at[NY - 1, pl.ds(B, B)], b3_send))
    got(pf_ref.at[pl.ds(0, NX - 1)], f3_send)
    got(pf_ref.at[NX - 1, 0], f3_send)
    pl.when(jnp.logical_not(relay))(lambda: got(pf_ref.at[NX - 1, 1], f3_send))

    got(rf_ref, f3_recv)
    total = rf_ref[0, 0]
    for i in range(1, NX * 2):
        total += rf_ref[i // 2, i % 2]
    resp_ref[...] = total.astype(BF16)

    got(rb_ref, b3_recv)
    total = rb_ref[0]
    for i in range(1, NY):
        total += rb_ref[i]
    grad_ref[...] = total.astype(BF16)


def solution(mesh):
    ns = mesh.shape["sp"]

    def local(activations, weights, out_grad):
        act = activations.reshape(2 * B, LANES)
        grad = out_grad.reshape(B, -1)
        wide = grad.shape[1]
        w = jnp.swapaxes(weights, 3, 4).reshape(27, B, 2 * B)
        dma = pltpu.SemaphoreType.DMA
        responses, in_grad = pl.pallas_call(
            functools.partial(kernel, ns),
            out_shape=(
                pltpu.VMEM((B, wide), BF16),
                pltpu.VMEM((2 * B, LANES), BF16),
            ),
            in_specs=[pl.BlockSpec(memory_space=pl.ANY)] * 3,
            out_specs=(pl.BlockSpec(memory_space=pltpu.VMEM),) * 2,
            scratch_shapes=[
                pltpu.VMEM((3, 2 * B, LANES), BF16),
                pltpu.VMEM((B, wide), BF16),
                pltpu.VMEM((27, B, 2 * B), BF16),
                pltpu.VMEM((NY, 3, 2 * B, LANES), BF16),
                pltpu.VMEM((2, 3, 2, 2 * B, wide), BF16),
                pltpu.VMEM((3, 2 * B, LANES), BF16),
                pltpu.VMEM((3, 2 * B, LANES), BF16),
                pltpu.VMEM((2, 3, 2, 9, B, LANES), BF16),
                pltpu.VMEM((192, 768), BF16),
                pltpu.VMEM((192, 768), BF16),
                pltpu.VMEM((768, NY * LANES), BF16),
                pltpu.VMEM((768, NY * LANES), BF16),
                pltpu.VMEM((NY, 2 * B, LANES), F32),
                pltpu.VMEM((NX, 2, B, wide), F32),
                pltpu.VMEM((NY, 2 * B, LANES), F32),
                pltpu.VMEM((NX, 2, B, wide), F32),
                dma((3,)),
                dma((2,)), dma((2,)),
                dma((3,)), dma((3,)),
                dma((3,)), dma((3,)),
                dma((3,)), dma((2, 3)),
                dma((3,)), dma((3,)),
                dma((2,)), dma((2,)),
                dma, dma,
                dma, dma,
            ],
            compiler_params=pltpu.CompilerParams(
                collective_id=0, has_side_effects=True, vmem_limit_bytes=60 * 1024 * 1024,
            ),
        )(act, w, grad)
        return responses.reshape(out_grad.shape), in_grad.reshape(activations.shape)

    return jax.shard_map(
        local,
        mesh=mesh,
        in_specs=(
            P("chan", "sp", "filt"),
            P(None, None, None, "chan", "filt"),
            P("filt", "sp", "chan"),
        ),
        out_specs=(P("filt", "sp", "chan"), P("chan", "sp", "filt")),
        check_vma=False,
    )
```

```python
import functools

import jax
import jax.numpy as jnp
from jax import lax
from jax.experimental import pallas as pl
from jax.experimental.pallas import tpu as pltpu
from jax.sharding import PartitionSpec as P

MESH = pl.DeviceIdType.MESH
BF16 = jnp.bfloat16
F32 = jnp.float32
B = 32
NX, NY = 4, 8
FAR = (4, 3, 5, 2, 6, 1, 7)
LANES = 128


def kernel(
    ns,
    act_hbm, w_hbm, og_hbm, resp_ref, grad_ref,
    a_ref, o_ref, w_ref, d_ref, g_ref, hd_ref, hg_ref, wr_ref, lf_ref, lb_ref, rg_ref, rd_ref,
    pb_ref, pf_ref, rb_ref, rf_ref,
    load_sem, f1_send, f1_recv, f2_send, f2_recv, b1_send, b1_recv, b2_send, b2_recv,
    ws_send, ws_recv, h_send, h_recv, b3_send, b3_recv, f3_send, f3_recv, up_sem,
):
    chan, filt, s = lax.axis_index("chan"), lax.axis_index("filt"), lax.axis_index("sp")
    x, core = chan // 2, chan % 2
    zl, y = filt // NY, filt % NY
    k, xi = x // 2, x % 2
    other = 1 - core
    has_low, has_high = s > 0, s < ns - 1
    relay = core == k
    stays = core == zl

    def dev(x_, core_, zl_, y_, s_):
        return (x_ * 2 + core_, zl_ * NY + y_, s_)

    def remote(src, dst, ssem, rsem, to):
        return pltpu.make_async_remote_copy(
            src_ref=src, dst_ref=dst, send_sem=ssem, recv_sem=rsem,
            device_id=to, device_id_type=MESH,
        )

    def got(ref, sem):
        pltpu.make_async_copy(ref, ref, sem).wait()

    def start(args, own=None):
        if own is None:
            remote(*args).start()
            return
        pl.when(jnp.logical_not(own))(lambda: remote(*args).start())
        pl.when(own)(lambda: pltpu.make_async_copy(args[0], args[1], args[3]).start())

    def finish(args, own=None):
        if own is None:
            remote(*args).wait_send()
        else:
            pl.when(jnp.logical_not(own))(lambda: remote(*args).wait_send())

    barrier = pltpu.get_barrier_semaphore()

    def greet(to, sem=barrier):
        pl.semaphore_signal(sem, inc=1, device_id=to, device_id_type=MESH)

    loads = [
        pltpu.make_async_copy(act_hbm, a_ref.at[1], load_sem.at[0]),
        pltpu.make_async_copy(og_hbm, o_ref, load_sem.at[1]),
        pltpu.make_async_copy(w_hbm, w_ref, load_sem.at[2]),
    ]
    for load in loads:
        load.start()
    for d in FAR:
        for c in range(2):
            greet(dev(x, c, core, (y + d) % NY, s))

    def greet_slab(ds):
        for dc in range(2):
            for dz in range(2):
                if (ds, dc, dz) != (0, 0, 0):
                    greet(dev(x, (core + dc) % 2, (zl + dz) % 2, y, s + ds))

    pl.when(has_high)(lambda: greet_slab(1))
    greet_slab(0)
    for d in range(1, NX):
        greet(dev((x + d) % NX, core, zl, y, s))

    def clear_planes(p):
        d_ref[:, p] = jnp.zeros((NY,) + d_ref.shape[2:], BF16)

        @pl.when(relay)
        def _():
            g_ref[xi, p] = jnp.zeros(g_ref.shape[2:], BF16)

    pl.when(jnp.logical_not(has_low))(lambda: clear_planes(0))
    pl.when(jnp.logical_not(has_high))(lambda: clear_planes(2))
    loads[0].wait()
    loads[1].wait()
    count = 2 * (NY - 1) + 3 + (NX - 1)
    pl.semaphore_wait(barrier, count + 4 * has_low.astype(jnp.int32))

    @pl.when(has_low)
    def _():
        for dc in range(2):
            for dz in range(2):
                greet(dev(x, (core + dc) % 2, (zl + dz) % 2, y, s - 1), up_sem)

    def f1_copy(ds):
        return (a_ref.at[1], a_ref.at[1 - ds], f1_send.at[(ds + 1) // 2], f1_recv.at[(1 - ds) // 2],
                dev(x, core, zl, y, s + ds))

    def f2_sends(p, across):
        for d in (0,) + FAR:
            for dz in across:
                z2, y2 = (zl + dz) % 2, (y + d) % NY
                start((a_ref.at[p, pl.ds(z2 * B, B), :], d_ref.at[y, p, pl.ds(core * B, B), :],
                       f2_send.at[p], f2_recv.at[p], dev(x, zl, z2, y2, s)),
                      stays if (d, dz) == (0, 0) else None)

    def f2_finish(p):
        got(d_ref.at[pl.ds(0, NY - 1), p], f2_send.at[p])
        got(d_ref.at[NY - 1, p, pl.ds(0, B)], f2_send.at[p])
        pl.when(jnp.logical_not(stays))(lambda: got(d_ref.at[NY - 1, p, pl.ds(B, B)], f2_send.at[p]))

    def b1_copy(ds, dz):
        z2 = (zl + dz) % 2
        return (
            o_ref,
            g_ref.at[xi, 1 - ds, core, pl.ds(zl * B, B), :],
            b1_send.at[ds + 1], b1_recv.at[1 - ds], dev(x, k, z2, y, s + ds),
        )

    def b1_sends(ds):
        for dz in range(2):
            start(b1_copy(ds, dz), relay if (ds, dz) == (0, 0) else None)

    pl.when(has_low)(lambda: start(f1_copy(-1)))
    pl.when(has_low)(lambda: b1_sends(-1))
    b1_sends(0)
    f2_sends(1, (0, 1))

    loads[2].wait()
    blank = jnp.zeros((B, B), BF16)
    for h in range(2):
        slot = jnp.where(zl == h, h, 2)
        for a in range(3):
            for e in range(3):
                taps = [w_ref[a * 9 + b * 3 + e] for b in range(3)]
                wr_ref[core, slot, 0, a * 3 + e] = jnp.concatenate(
                    [t[:, h * B:(h + 1) * B] for t in taps] + [blank], axis=1)
    w_across = (wr_ref.at[core, 2, 0], wr_ref.at[core, zl, 0], ws_send.at[0], ws_recv.at[0], dev(x, core, 1 - zl, y, s))
    w_own = (wr_ref.at[core, zl], wr_ref.at[core, zl], ws_send.at[1], ws_recv.at[1], dev(x, other, zl, y, s))
    w_next = (wr_ref.at[core, 1 - zl], wr_ref.at[core, 1 - zl], ws_send.at[2], ws_recv.at[2], dev(x, other, zl, y, s))
    start(w_across)

    def turn(slot):
        for i in range(9):
            flip = wr_ref[core, slot, 0, i].astype(F32).T
            wr_ref[core, slot, 1, i] = jnp.concatenate(
                [flip[(2 - b) * B:(3 - b) * B] for b in range(3)] + [flip[3 * B:]], axis=1).astype(BF16)

    @pl.when(has_high)
    def _():
        pl.semaphore_wait(up_sem, 4)
        start(f1_copy(1))
        b1_sends(1)

    def b2_copy(p, d):
        return (g_ref.at[xi, p], g_ref.at[xi, p], b2_send.at[p], b2_recv.at[xi, p],
                dev((x + d) % NX, core, zl, y, s))

    def b2_sends(p):
        for d in (2, 1, 3):
            start(b2_copy(p, d))

    @pl.when(relay)
    def _():
        got(g_ref.at[xi, 1], b1_recv.at[1])
        b2_sends(1)

    @pl.when(has_low)
    def _():
        got(a_ref.at[0], f1_recv.at[0])
        f2_sends(0, (0, 1))

    @pl.when(has_high)
    def _():
        got(a_ref.at[2], f1_recv.at[1])
        f2_sends(2, (0, 1))

    @pl.when(relay)
    def _():
        pl.when(has_low)(lambda: got(g_ref.at[xi, 0], b1_recv.at[0]))
        b2_sends(0)
        pl.when(has_high)(lambda: got(g_ref.at[xi, 2], b1_recv.at[2]))
        b2_sends(2)

    turn(zl)
    start(w_own)
    got(wr_ref.at[core, 1 - zl, 0], ws_recv.at[0])
    turn(1 - zl)
    start(w_next)

    def low_g(p):
        return (g_ref.at[0, p, 0, :, pl.ds(0, LANES)], hg_ref.at[p], h_send.at[p], h_recv.at[p], dev(x, other, zl, y, s))

    def high_g(p):
        return (g_ref.at[1, p, 1, :, pl.ds(LANES, LANES)], hg_ref.at[p], h_send.at[p], h_recv.at[p], dev(x, other, zl, y, s))

    low_d = (d_ref.at[0], hd_ref, h_send.at[3], h_recv.at[3], dev(x, other, zl, y, s))
    high_d = (d_ref.at[NY - 1], hd_ref, h_send.at[3], h_recv.at[3], dev(x, other, zl, y, s))

    remote(*w_own).wait_recv()
    remote(*w_next).wait_recv()
    for cs in range(2):
        for z in range(2):
            for a in range(3):
                for e in range(3):
                    lf_ref[e * 64 + z * B:e * 64 + z * B + B, a * 256 + cs * 128:a * 256 + cs * 128 + 128] = (
                        wr_ref[cs, z, 0, a * 3 + e])
                    lb_ref[e * 64 + cs * B:e * 64 + cs * B + B, a * 256 + z * 128:a * 256 + z * 128 + 128] = (
                        wr_ref[cs, z, 1, (2 - a) * 3 + 2 - e])

    lane = lax.broadcasted_iota(jnp.int32, (64, LANES), 1)
    left_half = lane < 64
    inside_low = lane % 64 != 0
    inside_high = lane % 64 != 63

    def put(r_ref, a, b, t, tile):
        for c in range(2):
            row = a * 256 + c * 128 + b * B
            r_ref[row:row + B, t * LANES:(t + 1) * LANES] = tile[c * B:(c + 1) * B]

    def half_turn(tile):
        return pltpu.roll(tile.astype(F32), 64, axis=1)

    def rows(r_ref, a, tile_of):
        for c in range(2):
            row = a * 256 + c * 128 + 3 * B
            r_ref[row:row + B, :] = jnp.zeros((B, r_ref.shape[1]), BF16)
        turned = None
        for t in range(NY):
            tile = tile_of(a, t)
            put(r_ref, a, 1, t, tile)
            before, turned = turned, half_turn(tile)
            if t > 0:
                mid = jnp.where(left_half, before, turned).astype(BF16)
                put(r_ref, a, 0, t, mid)
                put(r_ref, a, 2, t - 1, mid)

    def edge_rows(r_ref, a, tile_of, halo):
        turned = half_turn(halo)
        none = jnp.zeros_like(turned)
        low = jnp.where(core == 1, turned, none)
        high = jnp.where(core == 0, turned, none)
        put(r_ref, a, 0, 0, jnp.where(left_half, low, half_turn(tile_of(a, 0))).astype(BF16))
        put(r_ref, a, 2, NY - 1, jnp.where(left_half, half_turn(tile_of(a, NY - 1)), high).astype(BF16))

    def multiply(l_ref, r_ref, pair, emit):
        part = jnp.dot(l_ref[...], r_ref[:, pair * 256:(pair + 1) * 256], preferred_element_type=F32)
        for h in range(2):
            piece = part[:, h * LANES:(h + 1) * LANES]
            total = piece[64:128]
            total += jnp.where(inside_low, pltpu.roll(piece[0:64], 1, axis=1), 0.0)
            total += jnp.where(inside_high, pltpu.roll(piece[128:192], LANES - 1, axis=1), 0.0)
            emit(pair * 2 + h, total)

    def g_tile(a, t):
        return g_ref[t // 4, a, t // 2 % 2, :, t % 2 * LANES:(t % 2 + 1) * LANES]

    def emit_b(t, total):
        pb_ref[t] = total

    def b3_sends(tiles):
        for t in tiles:
            for dc in range(2):
                c2 = (core + dc) % 2
                start((pb_ref.at[t, pl.ds(c2 * B, B), :], rb_ref.at[y, pl.ds(zl * B, B), :],
                       b3_send, b3_recv, dev(x, c2, core, t, s)),
                      jnp.logical_and(stays, y == t) if dc == 0 else None)

    for p in (1, 0, 2):
        for i in range(2):
            @pl.when(jnp.logical_not(jnp.logical_and(relay, xi == i)))
            def _(i=i, p=p):
                got(g_ref.at[i, p], b2_recv.at[i, p])

        pl.when(core == 0)(lambda: start(high_g(p)))
        pl.when(core == 1)(lambda: start(low_g(p)))
        rows(rg_ref, p, g_tile)
    for pair in (1, 2):
        multiply(lb_ref, rg_ref, pair, emit_b)
    got(d_ref.at[:, 1], f2_recv.at[1])
    b3_sends((4, 3, 5, 2))
    for p in range(3):
        got(hg_ref.at[p], h_recv.at[p])
        edge_rows(rg_ref, p, g_tile, hg_ref[p])
    for pair in (0, 3):
        multiply(lb_ref, rg_ref, pair, emit_b)
    b3_sends((0, 7, 1, 6))

    def d_tile(a, t):
        return d_ref[t, a]

    rows(rd_ref, 1, d_tile)
    pl.when(has_low)(lambda: got(d_ref.at[:, 0], f2_recv.at[0]))
    pl.when(has_high)(lambda: got(d_ref.at[:, 2], f2_recv.at[2]))
    pl.when(core == 0)(lambda: start(high_d))
    pl.when(core == 1)(lambda: start(low_d))
    rows(rd_ref, 0, d_tile)
    rows(rd_ref, 2, d_tile)

    def emit_f(t, total):
        for z in range(2):
            pf_ref[t // 2, z, :, t % 2 * LANES:(t % 2 + 1) * LANES] = total[z * B:(z + 1) * B]

    def f3_sends(j):
        for dz in range(2):
            x2, c2, z2 = core * 2 + j // 2, j % 2, (zl + dz) % 2
            own = jnp.logical_and(x2 == x, c2 == core) if dz == 0 else None
            start((pf_ref.at[j, z2], rf_ref.at[x, zl], f3_send, f3_recv, dev(x2, c2, z2, y, s)), own)

    for pair in (1, 2):
        multiply(lf_ref, rd_ref, pair, emit_f)
        f3_sends(pair)
    pl.when(core == 0)(lambda: remote(*low_d).wait_recv())
    pl.when(core == 1)(lambda: remote(*high_d).wait_recv())
    for a in range(3):
        edge_rows(rd_ref, a, d_tile, hd_ref[a])
    for pair in (0, 3):
        multiply(lf_ref, rd_ref, pair, emit_f)
        f3_sends(pair)

    pl.when(has_low)(lambda: finish(f1_copy(-1)))
    pl.when(has_high)(lambda: finish(f1_copy(1)))
    pair = g_ref.at[0, 0, 0]
    pl.when(has_low)(lambda: got(pair, b1_send.at[0]))
    pl.when(has_high)(lambda: got(pair, b1_send.at[2]))
    pl.when(relay)(lambda: got(pair.at[pl.ds(0, B)], b1_send.at[1]))
    pl.when(jnp.logical_not(relay))(lambda: got(pair, b1_send.at[1]))
    f2_finish(1)
    pl.when(has_low)(lambda: f2_finish(0))
    pl.when(has_high)(lambda: f2_finish(2))
    for copy in (w_across, w_own, w_next):
        finish(copy)

    @pl.when(relay)
    def _():
        for p in range(3):
            got(g_ref.at[0], b2_send.at[p])

    for p in range(3):
        got(hg_ref.at[p], h_send.at[p])
    pl.when(core == 0)(lambda: finish(high_d))
    pl.when(core == 1)(lambda: finish(low_d))
    got(pb_ref.at[pl.ds(0, NY - 1)], b3_send)
    got(pb_ref.at[NY - 1, pl.ds(0, B)], b3_send)
    pl.when(jnp.logical_not(stays))(lambda: got(pb_ref.at[NY - 1, pl.ds(B, B)], b3_send))
    got(pf_ref.at[pl.ds(0, NX - 1)], f3_send)
    got(pf_ref.at[NX - 1, 0], f3_send)
    pl.when(jnp.logical_not(relay))(lambda: got(pf_ref.at[NX - 1, 1], f3_send))

    got(rf_ref, f3_recv)
    total = rf_ref[0, 0]
    for i in range(1, NX * 2):
        total += rf_ref[i // 2, i % 2]
    resp_ref[...] = total.astype(BF16)

    got(rb_ref, b3_recv)
    total = rb_ref[0]
    for i in range(1, NY):
        total += rb_ref[i]
    grad_ref[...] = total.astype(BF16)


def solution(mesh):
    ns = mesh.shape["sp"]

    def local(activations, weights, out_grad):
        act = activations.reshape(2 * B, LANES)
        grad = out_grad.reshape(B, -1)
        wide = grad.shape[1]
        w = jnp.swapaxes(weights, 3, 4).reshape(27, B, 2 * B)
        dma = pltpu.SemaphoreType.DMA
        responses, in_grad = pl.pallas_call(
            functools.partial(kernel, ns),
            out_shape=(
                pltpu.VMEM((B, wide), BF16),
                pltpu.VMEM((2 * B, LANES), BF16),
            ),
            in_specs=[pl.BlockSpec(memory_space=pl.ANY)] * 3,
            out_specs=(pl.BlockSpec(memory_space=pltpu.VMEM),) * 2,
            scratch_shapes=[
                pltpu.VMEM((3, 2 * B, LANES), BF16),
                pltpu.VMEM((B, wide), BF16),
                pltpu.VMEM((27, B, 2 * B), BF16),
                pltpu.VMEM((NY, 3, 2 * B, LANES), BF16),
                pltpu.VMEM((2, 3, 2, 2 * B, wide), BF16),
                pltpu.VMEM((3, 2 * B, LANES), BF16),
                pltpu.VMEM((3, 2 * B, LANES), BF16),
                pltpu.VMEM((2, 3, 2, 9, B, LANES), BF16),
                pltpu.VMEM((192, 768), BF16),
                pltpu.VMEM((192, 768), BF16),
                pltpu.VMEM((768, NY * LANES), BF16),
                pltpu.VMEM((768, NY * LANES), BF16),
                pltpu.VMEM((NY, 2 * B, LANES), F32),
                pltpu.VMEM((NX, 2, B, wide), F32),
                pltpu.VMEM((NY, 2 * B, LANES), F32),
                pltpu.VMEM((NX, 2, B, wide), F32),
                dma((3,)),
                dma((2,)), dma((2,)),
                dma((3,)), dma((3,)),
                dma((3,)), dma((3,)),
                dma((3,)), dma((2, 3)),
                dma((3,)), dma((3,)),
                dma((4,)), dma((4,)),
                dma, dma,
                dma, dma,
                pltpu.SemaphoreType.REGULAR,
            ],
            compiler_params=pltpu.CompilerParams(
                collective_id=0, has_side_effects=True, vmem_limit_bytes=60 * 1024 * 1024,
            ),
        )(act, w, grad)
        return responses.reshape(out_grad.shape), in_grad.reshape(activations.shape)

    return jax.shard_map(
        local,
        mesh=mesh,
        in_specs=(
            P("chan", "sp", "filt"),
            P(None, None, None, "chan", "filt"),
            P("filt", "sp", "chan"),
        ),
        out_specs=(P("filt", "sp", "chan"), P("chan", "sp", "filt")),
        check_vma=False,
    )
```

```python
import functools

import jax
import jax.numpy as jnp
from jax import lax
from jax.experimental import pallas as pl
from jax.experimental.pallas import tpu as pltpu
from jax.sharding import PartitionSpec as P

MESH = pl.DeviceIdType.MESH
BF16 = jnp.bfloat16
F32 = jnp.float32
B = 32
NX, NY = 4, 8
FAR = (4, 3, 5, 2, 6, 1, 7)
LANES = 128


def kernel(
    ns,
    act_hbm, w_hbm, og_hbm, resp_ref, grad_ref,
    a_ref, o_ref, w_ref, d_ref, g_ref, hd_ref, hg_ref, wr_ref, lf_ref, lb_ref, rg_ref, rd_ref,
    pb_ref, pf_ref, rb_ref, rf_ref,
    load_sem, sent, f1_recv, f2_recv, b1_recv, b2_recv, ws_recv, h_recv, b3_recv, f3_recv, up_sem,
):
    chan, filt, s = lax.axis_index("chan"), lax.axis_index("filt"), lax.axis_index("sp")
    x, core = chan // 2, chan % 2
    zl, y = filt // NY, filt % NY
    k, xi = x // 2, x % 2
    other = 1 - core
    has_low, has_high = s > 0, s < ns - 1
    relay = core == k
    stays = core == zl

    def dev(x_, core_, zl_, y_, s_):
        return (x_ * 2 + core_, zl_ * NY + y_, s_)

    def remote(src, dst, ssem, rsem, to):
        return pltpu.make_async_remote_copy(
            src_ref=src, dst_ref=dst, send_sem=ssem, recv_sem=rsem,
            device_id=to, device_id_type=MESH,
        )

    def got(ref, sem):
        pltpu.make_async_copy(ref, ref, sem).wait()

    def start(args, own=None):
        if own is None:
            remote(*args).start()
            return
        pl.when(jnp.logical_not(own))(lambda: remote(*args).start())
        pl.when(own)(lambda: pltpu.make_async_copy(args[0], args[1], args[3]).start())

    def finish(args, own=None):
        if own is None:
            remote(*args).wait_send()
        else:
            pl.when(jnp.logical_not(own))(lambda: remote(*args).wait_send())

    barrier = pltpu.get_barrier_semaphore()

    def greet(to, sem=barrier):
        pl.semaphore_signal(sem, inc=1, device_id=to, device_id_type=MESH)

    loads = [
        pltpu.make_async_copy(act_hbm, a_ref.at[1], load_sem.at[0]),
        pltpu.make_async_copy(og_hbm, o_ref, load_sem.at[1]),
        pltpu.make_async_copy(w_hbm, w_ref, load_sem.at[2]),
    ]
    for load in loads:
        load.start()
    for d in FAR:
        for c in range(2):
            greet(dev(x, c, core, (y + d) % NY, s))

    def greet_slab(ds):
        for dc in range(2):
            for dz in range(2):
                if (ds, dc, dz) != (0, 0, 0):
                    greet(dev(x, (core + dc) % 2, (zl + dz) % 2, y, s + ds))

    pl.when(has_high)(lambda: greet_slab(1))
    greet_slab(0)
    for d in range(1, NX):
        greet(dev((x + d) % NX, core, zl, y, s))

    def clear_planes(p):
        d_ref[:, p] = jnp.zeros((NY,) + d_ref.shape[2:], BF16)

        @pl.when(relay)
        def _():
            g_ref[xi, p] = jnp.zeros(g_ref.shape[2:], BF16)

    pl.when(jnp.logical_not(has_low))(lambda: clear_planes(0))
    pl.when(jnp.logical_not(has_high))(lambda: clear_planes(2))
    loads[0].wait()
    loads[1].wait()
    count = 2 * (NY - 1) + 3 + (NX - 1)
    pl.semaphore_wait(barrier, count + 4 * has_low.astype(jnp.int32))

    @pl.when(has_low)
    def _():
        for dc in range(2):
            for dz in range(2):
                greet(dev(x, (core + dc) % 2, (zl + dz) % 2, y, s - 1), up_sem)

    def f1_copy(ds):
        return (a_ref.at[1], a_ref.at[1 - ds], sent, f1_recv.at[(1 - ds) // 2],
                dev(x, core, zl, y, s + ds))

    def f2_sends(p, across):
        for y2 in (0, 1, 7, 2, 6, 3, 5, 4):
            for dz in across:
                z2 = (zl + dz) % 2
                start((a_ref.at[p, pl.ds(z2 * B, B), :], d_ref.at[y, p, pl.ds(core * B, B), :],
                       sent, f2_recv.at[p], dev(x, zl, z2, y2, s)),
                      jnp.logical_and(stays, y == y2) if dz == 0 else None)

    def f2_finish(p):
        got(d_ref.at[pl.ds(0, NY - 1), p], sent)
        got(d_ref.at[NY - 1, p, pl.ds(0, B)], sent)
        pl.when(jnp.logical_not(stays))(lambda: got(d_ref.at[NY - 1, p, pl.ds(B, B)], sent))

    def b1_copy(ds, dz):
        z2 = (zl + dz) % 2
        return (
            o_ref,
            g_ref.at[xi, 1 - ds, core, pl.ds(zl * B, B), :],
            sent, b1_recv.at[1 - ds], dev(x, k, z2, y, s + ds),
        )

    def b1_sends(ds):
        for dz in range(2):
            start(b1_copy(ds, dz), relay if (ds, dz) == (0, 0) else None)

    pl.when(has_low)(lambda: start(f1_copy(-1)))
    pl.when(has_low)(lambda: b1_sends(-1))
    b1_sends(0)
    f2_sends(1, (0, 1))

    loads[2].wait()
    blank = jnp.zeros((B, B), BF16)
    for h in range(2):
        slot = jnp.where(zl == h, h, 2)
        for a in range(3):
            for e in range(3):
                taps = [w_ref[a * 9 + b * 3 + e] for b in range(3)]
                wr_ref[core, slot, 0, a * 3 + e] = jnp.concatenate(
                    [t[:, h * B:(h + 1) * B] for t in taps] + [blank], axis=1)
    w_across = (wr_ref.at[core, 2, 0], wr_ref.at[core, zl, 0], sent, ws_recv.at[0], dev(x, core, 1 - zl, y, s))
    w_own = (wr_ref.at[core, zl], wr_ref.at[core, zl], sent, ws_recv.at[1], dev(x, other, zl, y, s))
    w_next = (wr_ref.at[core, 1 - zl], wr_ref.at[core, 1 - zl], sent, ws_recv.at[2], dev(x, other, zl, y, s))
    start(w_across)

    def turn(slot):
        for i in range(9):
            flip = wr_ref[core, slot, 0, i].astype(F32).T
            wr_ref[core, slot, 1, i] = jnp.concatenate(
                [flip[(2 - b) * B:(3 - b) * B] for b in range(3)] + [flip[3 * B:]], axis=1).astype(BF16)

    @pl.when(has_high)
    def _():
        pl.semaphore_wait(up_sem, 4)
        b1_sends(1)
        start(f1_copy(1))

    def b2_copy(p, d):
        return (g_ref.at[xi, p], g_ref.at[xi, p], sent, b2_recv.at[xi, p],
                dev((x + d) % NX, core, zl, y, s))

    def b2_sends(p):
        for d in (2, 1, 3):
            start(b2_copy(p, d))

    @pl.when(relay)
    def _():
        got(g_ref.at[xi, 1], b1_recv.at[1])
        b2_sends(1)

    @pl.when(has_low)
    def _():
        got(a_ref.at[0], f1_recv.at[0])
        f2_sends(0, (0, 1))

    @pl.when(has_high)
    def _():
        got(a_ref.at[2], f1_recv.at[1])
        f2_sends(2, (0, 1))

    @pl.when(relay)
    def _():
        pl.when(has_low)(lambda: got(g_ref.at[xi, 0], b1_recv.at[0]))
        b2_sends(0)
        pl.when(has_high)(lambda: got(g_ref.at[xi, 2], b1_recv.at[2]))
        b2_sends(2)

    turn(zl)
    start(w_own)
    got(wr_ref.at[core, 1 - zl, 0], ws_recv.at[0])
    turn(1 - zl)
    start(w_next)

    def low_g(p):
        return (g_ref.at[0, p, 0, :, pl.ds(0, LANES)], hg_ref.at[p], sent, h_recv.at[p], dev(x, other, zl, y, s))

    def high_g(p):
        return (g_ref.at[1, p, 1, :, pl.ds(LANES, LANES)], hg_ref.at[p], sent, h_recv.at[p], dev(x, other, zl, y, s))

    def low_d(p):
        return (d_ref.at[0, p], hd_ref.at[p], sent, h_recv.at[3 + p], dev(x, other, zl, y, s))

    def high_d(p):
        return (d_ref.at[NY - 1, p], hd_ref.at[p], sent, h_recv.at[3 + p], dev(x, other, zl, y, s))

    remote(*w_own).wait_recv()
    remote(*w_next).wait_recv()
    for cs in range(2):
        for z in range(2):
            for a in range(3):
                for e in range(3):
                    lf_ref[e * 64 + z * B:e * 64 + z * B + B, a * 256 + cs * 128:a * 256 + cs * 128 + 128] = (
                        wr_ref[cs, z, 0, a * 3 + e])
                    lb_ref[e * 64 + cs * B:e * 64 + cs * B + B, a * 256 + z * 128:a * 256 + z * 128 + 128] = (
                        wr_ref[cs, z, 1, (2 - a) * 3 + 2 - e])

    lane = lax.broadcasted_iota(jnp.int32, (64, LANES), 1)
    left_half = lane < 64
    inside_low = lane % 64 != 0
    inside_high = lane % 64 != 63

    def put(r_ref, a, b, t, tile):
        for c in range(2):
            row = a * 256 + c * 128 + b * B
            r_ref[row:row + B, t * LANES:(t + 1) * LANES] = tile[c * B:(c + 1) * B]

    def half_turn(tile):
        return pltpu.roll(tile.astype(F32), 64, axis=1)

    def rows(r_ref, a, tile_of):
        for c in range(2):
            row = a * 256 + c * 128 + 3 * B
            r_ref[row:row + B, :] = jnp.zeros((B, r_ref.shape[1]), BF16)
        turned = None
        for t in range(NY):
            tile = tile_of(a, t)
            put(r_ref, a, 1, t, tile)
            before, turned = turned, half_turn(tile)
            if t > 0:
                mid = jnp.where(left_half, before, turned).astype(BF16)
                put(r_ref, a, 0, t, mid)
                put(r_ref, a, 2, t - 1, mid)

    def edge_rows(r_ref, a, tile_of, halo):
        turned = half_turn(halo)
        none = jnp.zeros_like(turned)
        low = jnp.where(core == 1, turned, none)
        high = jnp.where(core == 0, turned, none)
        put(r_ref, a, 0, 0, jnp.where(left_half, low, half_turn(tile_of(a, 0))).astype(BF16))
        put(r_ref, a, 2, NY - 1, jnp.where(left_half, half_turn(tile_of(a, NY - 1)), high).astype(BF16))

    def multiply(l_ref, r_ref, pair, emit):
        part = jnp.dot(l_ref[...], r_ref[:, pair * 256:(pair + 1) * 256], preferred_element_type=F32)
        for h in range(2):
            piece = part[:, h * LANES:(h + 1) * LANES]
            total = piece[64:128]
            total += jnp.where(inside_low, pltpu.roll(piece[0:64], 1, axis=1), 0.0)
            total += jnp.where(inside_high, pltpu.roll(piece[128:192], LANES - 1, axis=1), 0.0)
            emit(pair * 2 + h, total)

    def g_tile(a, t):
        return g_ref[t // 4, a, t // 2 % 2, :, t % 2 * LANES:(t % 2 + 1) * LANES]

    def emit_b(t, total):
        pb_ref[t] = total

    def b3_sends(tiles):
        for t in tiles:
            for dc in range(2):
                c2 = (core + dc) % 2
                start((pb_ref.at[t, pl.ds(c2 * B, B), :], rb_ref.at[y, pl.ds(zl * B, B), :],
                       sent, b3_recv, dev(x, c2, core, t, s)),
                      jnp.logical_and(stays, y == t) if dc == 0 else None)

    for p in (1, 0, 2):
        for i in range(2):
            @pl.when(jnp.logical_not(jnp.logical_and(relay, xi == i)))
            def _(i=i, p=p):
                got(g_ref.at[i, p], b2_recv.at[i, p])

        pl.when(core == 0)(lambda: start(high_g(p)))
        pl.when(core == 1)(lambda: start(low_g(p)))
        rows(rg_ref, p, g_tile)
    for n, pair in enumerate((1,)):
        multiply(lb_ref, rg_ref, pair, emit_b)
        if n == 0:
            got(d_ref.at[:, 1], f2_recv.at[1])
        b3_sends((2 * pair, 2 * pair + 1))
    for p in range(3):
        got(hg_ref.at[p], h_recv.at[p])
        edge_rows(rg_ref, p, g_tile, hg_ref[p])
    for pair in (0, 3, 2):
        multiply(lb_ref, rg_ref, pair, emit_b)
        b3_sends((2 * pair, 2 * pair + 1))

    def d_tile(a, t):
        return d_ref[t, a]

    for p in (1, 0, 2):
        if p == 0:
            pl.when(has_low)(lambda: got(d_ref.at[:, 0], f2_recv.at[0]))
        if p == 2:
            pl.when(has_high)(lambda: got(d_ref.at[:, 2], f2_recv.at[2]))
        pl.when(core == 0)(lambda: start(high_d(p)))
        pl.when(core == 1)(lambda: start(low_d(p)))
        rows(rd_ref, p, d_tile)

    def emit_f(t, total):
        for z in range(2):
            pf_ref[t // 2, z, :, t % 2 * LANES:(t % 2 + 1) * LANES] = total[z * B:(z + 1) * B]

    def f3_sends(j):
        for dz in range(2):
            x2, c2, z2 = core * 2 + j // 2, j % 2, (zl + dz) % 2
            own = jnp.logical_and(x2 == x, c2 == core) if dz == 0 else None
            start((pf_ref.at[j, z2], rf_ref.at[x, zl], sent, f3_recv, dev(x2, c2, z2, y, s)), own)

    for pair in (1,):
        multiply(lf_ref, rd_ref, pair, emit_f)
        f3_sends(pair)
    for p in range(3):
        got(hd_ref.at[p], h_recv.at[3 + p])
        edge_rows(rd_ref, p, d_tile, hd_ref[p])
    for pair in (0, 2, 3):
        multiply(lf_ref, rd_ref, pair, emit_f)
        f3_sends(pair)

    pl.when(has_low)(lambda: finish(f1_copy(-1)))
    pl.when(has_high)(lambda: finish(f1_copy(1)))
    pair = g_ref.at[0, 0, 0]
    pl.when(has_low)(lambda: got(pair, sent))
    pl.when(has_high)(lambda: got(pair, sent))
    pl.when(relay)(lambda: got(pair.at[pl.ds(0, B)], sent))
    pl.when(jnp.logical_not(relay))(lambda: got(pair, sent))
    f2_finish(1)
    pl.when(has_low)(lambda: f2_finish(0))
    pl.when(has_high)(lambda: f2_finish(2))
    for copy in (w_across, w_own, w_next):
        finish(copy)

    @pl.when(relay)
    def _():
        for p in range(3):
            got(g_ref.at[0], sent)

    for p in range(3):
        got(hg_ref.at[p], sent)
    for p in range(3):
        got(hd_ref.at[p], sent)
    got(pb_ref.at[pl.ds(0, NY - 1)], sent)
    got(pb_ref.at[NY - 1, pl.ds(0, B)], sent)
    pl.when(jnp.logical_not(stays))(lambda: got(pb_ref.at[NY - 1, pl.ds(B, B)], sent))
    got(pf_ref.at[pl.ds(0, NX - 1)], sent)
    got(pf_ref.at[NX - 1, 0], sent)
    pl.when(jnp.logical_not(relay))(lambda: got(pf_ref.at[NX - 1, 1], sent))

    got(rf_ref, f3_recv)
    total = rf_ref[0, 0]
    for i in range(1, NX * 2):
        total += rf_ref[i // 2, i % 2]
    resp_ref[...] = total.astype(BF16)

    got(rb_ref, b3_recv)
    total = rb_ref[0]
    for i in range(1, NY):
        total += rb_ref[i]
    grad_ref[...] = total.astype(BF16)


def solution(mesh):
    ns = mesh.shape["sp"]

    def local(activations, weights, out_grad):
        act = activations.reshape(2 * B, LANES)
        grad = out_grad.reshape(B, -1)
        wide = grad.shape[1]
        w = jnp.swapaxes(weights, 3, 4).reshape(27, B, 2 * B)
        dma = pltpu.SemaphoreType.DMA
        responses, in_grad = pl.pallas_call(
            functools.partial(kernel, ns),
            out_shape=(
                pltpu.VMEM((B, wide), BF16),
                pltpu.VMEM((2 * B, LANES), BF16),
            ),
            in_specs=[pl.BlockSpec(memory_space=pl.ANY)] * 3,
            out_specs=(pl.BlockSpec(memory_space=pltpu.VMEM),) * 2,
            scratch_shapes=[
                pltpu.VMEM((3, 2 * B, LANES), BF16),
                pltpu.VMEM((B, wide), BF16),
                pltpu.VMEM((27, B, 2 * B), BF16),
                pltpu.VMEM((NY, 3, 2 * B, LANES), BF16),
                pltpu.VMEM((2, 3, 2, 2 * B, wide), BF16),
                pltpu.VMEM((3, 2 * B, LANES), BF16),
                pltpu.VMEM((3, 2 * B, LANES), BF16),
                pltpu.VMEM((2, 3, 2, 9, B, LANES), BF16),
                pltpu.VMEM((192, 768), BF16),
                pltpu.VMEM((192, 768), BF16),
                pltpu.VMEM((768, NY * LANES), BF16),
                pltpu.VMEM((768, NY * LANES), BF16),
                pltpu.VMEM((NY, 2 * B, LANES), F32),
                pltpu.VMEM((NX, 2, B, wide), F32),
                pltpu.VMEM((NY, 2 * B, LANES), F32),
                pltpu.VMEM((NX, 2, B, wide), F32),
                dma((3,)), dma,
                dma((2,)), dma((3,)), dma((3,)), dma((2, 3)), dma((3,)), dma((6,)),
                dma, dma,
                pltpu.SemaphoreType.REGULAR,
            ],
            compiler_params=pltpu.CompilerParams(
                collective_id=0, has_side_effects=True, vmem_limit_bytes=60 * 1024 * 1024,
            ),
        )(act, w, grad)
        return responses.reshape(out_grad.shape), in_grad.reshape(activations.shape)

    return jax.shard_map(
        local,
        mesh=mesh,
        in_specs=(
            P("chan", "sp", "filt"),
            P(None, None, None, "chan", "filt"),
            P("filt", "sp", "chan"),
        ),
        out_specs=(P("filt", "sp", "chan"), P("chan", "sp", "filt")),
        check_vma=False,
    )
```

```python
import functools

import jax
import jax.numpy as jnp
from jax import lax
from jax.experimental import pallas as pl
from jax.experimental.pallas import tpu as pltpu
from jax.sharding import PartitionSpec as P

MESH = pl.DeviceIdType.MESH
BF16 = jnp.bfloat16
F32 = jnp.float32
B = 32
NX, NY = 4, 8
FAR = (4, 3, 5, 2, 6, 1, 7)
ORDER = (0, 1, 7, 2, 6, 3, 5, 4)
LANES = 128


def kernel(
    ns,
    act_hbm, w_hbm, og_hbm, resp_ref, grad_ref,
    a_ref, o_ref, w_ref, d_ref, g_ref, hd_ref, hg_ref, wr_ref, lf_ref, lb_ref, rg_ref, rd_ref,
    pb_ref, pf_ref, rb_ref, rf_ref,
    load_sem, sent, f1_recv, f2_recv, b1_recv, b2_recv, ws_recv, h_recv, b3_recv, f3_recv, up_sem,
):
    chan, filt, s = lax.axis_index("chan"), lax.axis_index("filt"), lax.axis_index("sp")
    x, core = chan // 2, chan % 2
    zl, y = filt // NY, filt % NY
    k, xi = x // 2, x % 2
    other = 1 - core
    has_low, has_high = s > 0, s < ns - 1
    relay = core == k
    stays = core == zl

    def dev(x_, core_, zl_, y_, s_):
        return (x_ * 2 + core_, zl_ * NY + y_, s_)

    def remote(src, dst, ssem, rsem, to):
        return pltpu.make_async_remote_copy(
            src_ref=src, dst_ref=dst, send_sem=ssem, recv_sem=rsem,
            device_id=to, device_id_type=MESH,
        )

    def got(ref, sem):
        pltpu.make_async_copy(ref, ref, sem).wait()

    def start(args, own=None):
        if own is None:
            remote(*args).start()
            return
        pl.when(jnp.logical_not(own))(lambda: remote(*args).start())
        pl.when(own)(lambda: pltpu.make_async_copy(args[0], args[1], args[3]).start())

    def finish(args, own=None):
        if own is None:
            remote(*args).wait_send()
        else:
            pl.when(jnp.logical_not(own))(lambda: remote(*args).wait_send())

    barrier = pltpu.get_barrier_semaphore()

    def greet(to, sem=barrier):
        pl.semaphore_signal(sem, inc=1, device_id=to, device_id_type=MESH)

    loads = [
        pltpu.make_async_copy(act_hbm, a_ref, load_sem.at[0]),
        pltpu.make_async_copy(og_hbm, o_ref, load_sem.at[1]),
        pltpu.make_async_copy(w_hbm, w_ref, load_sem.at[2]),
    ]
    for load in loads:
        load.start()
    for d in FAR:
        greet(dev(x, core, zl, (y + d) % NY, s))

    def greet_slab(ds):
        for dc in range(2):
            for dz in range(2):
                if (ds, dc, dz) != (0, 0, 0):
                    greet(dev(x, (core + dc) % 2, (zl + dz) % 2, y, s + ds))

    pl.when(has_high)(lambda: greet_slab(1))
    greet_slab(0)
    for d in range(1, NX):
        greet(dev((x + d) % NX, core, zl, y, s))

    def clear_planes(p):
        d_ref[:, p] = jnp.zeros((NY,) + d_ref.shape[2:], BF16)

        @pl.when(relay)
        def _():
            g_ref[xi, p] = jnp.zeros(g_ref.shape[2:], BF16)

    pl.when(jnp.logical_not(has_low))(lambda: clear_planes(0))
    pl.when(jnp.logical_not(has_high))(lambda: clear_planes(2))
    loads[0].wait()
    loads[1].wait()
    count = (NY - 1) + 3 + (NX - 1)
    pl.semaphore_wait(barrier, count + 4 * has_low.astype(jnp.int32))

    @pl.when(has_low)
    def _():
        for dc in range(2):
            for dz in range(2):
                greet(dev(x, (core + dc) % 2, (zl + dz) % 2, y, s - 1), up_sem)

    def f1_sends(ds):
        for dz in range(2):
            z2 = (zl + dz) % 2
            start((a_ref.at[pl.ds(z2 * B, B), :], d_ref.at[y, 1 - ds, pl.ds(core * B, B), :],
                   sent, f1_recv.at[1 - ds], dev(x, zl, z2, y, s + ds)),
                  stays if (ds, dz) == (0, 0) else None)

    def f2_sends(p):
        for y2 in ORDER:
            @pl.when(y != y2)
            def _(y2=y2):
                start((d_ref.at[y, p], d_ref.at[y, p], sent, f2_recv.at[p], dev(x, core, zl, y2, s)))

    def b1_copy(ds, dz):
        z2 = (zl + dz) % 2
        return (
            o_ref,
            g_ref.at[xi, 1 - ds, core, pl.ds(zl * B, B), :],
            sent, b1_recv.at[1 - ds], dev(x, k, z2, y, s + ds),
        )

    def b1_sends(ds):
        for dz in range(2):
            start(b1_copy(ds, dz), relay if (ds, dz) == (0, 0) else None)

    pl.when(has_low)(lambda: f1_sends(-1))
    pl.when(has_low)(lambda: b1_sends(-1))
    f1_sends(0)
    b1_sends(0)

    loads[2].wait()
    blank = jnp.zeros((B, B), BF16)
    for h in range(2):
        slot = jnp.where(zl == h, h, 2)
        for a in range(3):
            for e in range(3):
                taps = [w_ref[a * 9 + b * 3 + e] for b in range(3)]
                wr_ref[core, slot, 0, a * 3 + e] = jnp.concatenate(
                    [t[:, h * B:(h + 1) * B] for t in taps] + [blank], axis=1)
    w_across = (wr_ref.at[core, 2, 0], wr_ref.at[core, zl, 0], sent, ws_recv.at[0], dev(x, core, 1 - zl, y, s))
    w_own = (wr_ref.at[core, zl], wr_ref.at[core, zl], sent, ws_recv.at[1], dev(x, other, zl, y, s))
    w_next = (wr_ref.at[core, 1 - zl], wr_ref.at[core, 1 - zl], sent, ws_recv.at[2], dev(x, other, zl, y, s))
    start(w_across)
    got(d_ref.at[y, 1], f1_recv.at[1])
    f2_sends(1)

    def turn(slot):
        for i in range(9):
            flip = wr_ref[core, slot, 0, i].astype(F32).T
            wr_ref[core, slot, 1, i] = jnp.concatenate(
                [flip[(2 - b) * B:(3 - b) * B] for b in range(3)] + [flip[3 * B:]], axis=1).astype(BF16)

    @pl.when(has_high)
    def _():
        pl.semaphore_wait(up_sem, 4)
        b1_sends(1)
        f1_sends(1)

    def b2_copy(p, d):
        return (g_ref.at[xi, p], g_ref.at[xi, p], sent, b2_recv.at[xi, p],
                dev((x + d) % NX, core, zl, y, s))

    def b2_sends(p):
        for d in (2, 1, 3):
            start(b2_copy(p, d))

    @pl.when(relay)
    def _():
        got(g_ref.at[xi, 1], b1_recv.at[1])
        b2_sends(1)

    @pl.when(has_low)
    def _():
        got(d_ref.at[y, 0], f1_recv.at[0])
        f2_sends(0)

    @pl.when(has_high)
    def _():
        got(d_ref.at[y, 2], f1_recv.at[2])
        f2_sends(2)

    @pl.when(relay)
    def _():
        pl.when(has_low)(lambda: got(g_ref.at[xi, 0], b1_recv.at[0]))
        b2_sends(0)
        pl.when(has_high)(lambda: got(g_ref.at[xi, 2], b1_recv.at[2]))
        b2_sends(2)

    turn(zl)
    start(w_own)
    got(wr_ref.at[core, 1 - zl, 0], ws_recv.at[0])
    turn(1 - zl)
    start(w_next)

    def low_g(p):
        return (g_ref.at[0, p, 0, :, pl.ds(0, LANES)], hg_ref.at[p], sent, h_recv.at[p], dev(x, other, zl, y, s))

    def high_g(p):
        return (g_ref.at[1, p, 1, :, pl.ds(LANES, LANES)], hg_ref.at[p], sent, h_recv.at[p], dev(x, other, zl, y, s))

    def low_d(p):
        return (d_ref.at[0, p], hd_ref.at[p], sent, h_recv.at[3 + p], dev(x, other, zl, y, s))

    def high_d(p):
        return (d_ref.at[NY - 1, p], hd_ref.at[p], sent, h_recv.at[3 + p], dev(x, other, zl, y, s))

    remote(*w_own).wait_recv()
    remote(*w_next).wait_recv()
    for cs in range(2):
        for z in range(2):
            for a in range(3):
                for e in range(3):
                    lf_ref[e * 64 + z * B:e * 64 + z * B + B, a * 256 + cs * 128:a * 256 + cs * 128 + 128] = (
                        wr_ref[cs, z, 0, a * 3 + e])
                    lb_ref[e * 64 + cs * B:e * 64 + cs * B + B, a * 256 + z * 128:a * 256 + z * 128 + 128] = (
                        wr_ref[cs, z, 1, (2 - a) * 3 + 2 - e])

    lane = lax.broadcasted_iota(jnp.int32, (64, LANES), 1)
    left_half = lane < 64
    inside_low = lane % 64 != 0
    inside_high = lane % 64 != 63

    def put(r_ref, a, b, t, tile):
        for c in range(2):
            row = a * 256 + c * 128 + b * B
            r_ref[row:row + B, t * LANES:(t + 1) * LANES] = tile[c * B:(c + 1) * B]

    def half_turn(tile):
        return pltpu.roll(tile.astype(F32), 64, axis=1)

    def rows(r_ref, a, tile_of):
        for c in range(2):
            row = a * 256 + c * 128 + 3 * B
            r_ref[row:row + B, :] = jnp.zeros((B, r_ref.shape[1]), BF16)
        turned = None
        for t in range(NY):
            tile = tile_of(a, t)
            put(r_ref, a, 1, t, tile)
            before, turned = turned, half_turn(tile)
            if t > 0:
                mid = jnp.where(left_half, before, turned).astype(BF16)
                put(r_ref, a, 0, t, mid)
                put(r_ref, a, 2, t - 1, mid)

    def edge_rows(r_ref, a, tile_of, halo):
        turned = half_turn(halo)
        none = jnp.zeros_like(turned)
        low = jnp.where(core == 1, turned, none)
        high = jnp.where(core == 0, turned, none)
        put(r_ref, a, 0, 0, jnp.where(left_half, low, half_turn(tile_of(a, 0))).astype(BF16))
        put(r_ref, a, 2, NY - 1, jnp.where(left_half, half_turn(tile_of(a, NY - 1)), high).astype(BF16))

    def multiply(l_ref, r_ref, pair, emit):
        part = jnp.dot(l_ref[...], r_ref[:, pair * 256:(pair + 1) * 256], preferred_element_type=F32)
        for h in range(2):
            piece = part[:, h * LANES:(h + 1) * LANES]
            total = piece[64:128]
            total += jnp.where(inside_low, pltpu.roll(piece[0:64], 1, axis=1), 0.0)
            total += jnp.where(inside_high, pltpu.roll(piece[128:192], LANES - 1, axis=1), 0.0)
            emit(pair * 2 + h, total)

    def g_tile(a, t):
        return g_ref[t // 4, a, t // 2 % 2, :, t % 2 * LANES:(t % 2 + 1) * LANES]

    def emit_b(t, total):
        pb_ref[t] = total

    def b3_sends(tiles):
        for t in tiles:
            for dc in range(2):
                c2 = (core + dc) % 2
                start((pb_ref.at[t, pl.ds(c2 * B, B), :], rb_ref.at[y, pl.ds(zl * B, B), :],
                       sent, b3_recv, dev(x, c2, core, t, s)),
                      jnp.logical_and(stays, y == t) if dc == 0 else None)

    for p in (1, 0, 2):
        for i in range(2):
            @pl.when(jnp.logical_not(jnp.logical_and(relay, xi == i)))
            def _(i=i, p=p):
                got(g_ref.at[i, p], b2_recv.at[i, p])

        pl.when(core == 0)(lambda: start(high_g(p)))
        pl.when(core == 1)(lambda: start(low_g(p)))
        rows(rg_ref, p, g_tile)
    multiply(lb_ref, rg_ref, 1, emit_b)
    got(d_ref.at[pl.ds(0, NY - 1), 1], f2_recv.at[1])
    b3_sends((2, 3))
    for p in range(3):
        got(hg_ref.at[p], h_recv.at[p])
        edge_rows(rg_ref, p, g_tile, hg_ref[p])
    for pair in (0, 3, 2):
        multiply(lb_ref, rg_ref, pair, emit_b)
        b3_sends((2 * pair, 2 * pair + 1))

    def d_tile(a, t):
        return d_ref[t, a]

    for p in (1, 0, 2):
        if p == 0:
            pl.when(has_low)(lambda: got(d_ref.at[pl.ds(0, NY - 1), 0], f2_recv.at[0]))
        if p == 2:
            pl.when(has_high)(lambda: got(d_ref.at[pl.ds(0, NY - 1), 2], f2_recv.at[2]))
        pl.when(core == 0)(lambda: start(high_d(p)))
        pl.when(core == 1)(lambda: start(low_d(p)))
        rows(rd_ref, p, d_tile)

    def emit_f(t, total):
        for z in range(2):
            pf_ref[t // 2, z, :, t % 2 * LANES:(t % 2 + 1) * LANES] = total[z * B:(z + 1) * B]

    def f3_sends(j):
        for dz in range(2):
            x2, c2, z2 = core * 2 + j // 2, j % 2, (zl + dz) % 2
            own = jnp.logical_and(x2 == x, c2 == core) if dz == 0 else None
            start((pf_ref.at[j, z2], rf_ref.at[x, zl], sent, f3_recv, dev(x2, c2, z2, y, s)), own)

    for pair in (1,):
        multiply(lf_ref, rd_ref, pair, emit_f)
        f3_sends(pair)
    for p in range(3):
        got(hd_ref.at[p], h_recv.at[3 + p])
        edge_rows(rd_ref, p, d_tile, hd_ref[p])
    for pair in (0, 2, 3):
        multiply(lf_ref, rd_ref, pair, emit_f)
        f3_sends(pair)

    pl.when(has_low)(lambda: got(a_ref, sent))
    pl.when(has_high)(lambda: got(a_ref, sent))
    got(a_ref.at[pl.ds(0, B)], sent)
    pl.when(jnp.logical_not(stays))(lambda: got(a_ref.at[pl.ds(B, B)], sent))
    pair = g_ref.at[0, 0, 0]
    pl.when(has_low)(lambda: got(pair, sent))
    pl.when(has_high)(lambda: got(pair, sent))
    pl.when(relay)(lambda: got(pair.at[pl.ds(0, B)], sent))
    pl.when(jnp.logical_not(relay))(lambda: got(pair, sent))
    got(d_ref.at[pl.ds(0, NY - 1), 1], sent)
    pl.when(has_low)(lambda: got(d_ref.at[pl.ds(0, NY - 1), 0], sent))
    pl.when(has_high)(lambda: got(d_ref.at[pl.ds(0, NY - 1), 2], sent))
    for copy in (w_across, w_own, w_next):
        finish(copy)

    @pl.when(relay)
    def _():
        for p in range(3):
            got(g_ref.at[0], sent)

    for p in range(3):
        got(hg_ref.at[p], sent)
    for p in range(3):
        got(hd_ref.at[p], sent)
    got(pb_ref.at[pl.ds(0, NY - 1)], sent)
    got(pb_ref.at[NY - 1, pl.ds(0, B)], sent)
    pl.when(jnp.logical_not(stays))(lambda: got(pb_ref.at[NY - 1, pl.ds(B, B)], sent))
    got(pf_ref.at[pl.ds(0, NX - 1)], sent)
    got(pf_ref.at[NX - 1, 0], sent)
    pl.when(jnp.logical_not(relay))(lambda: got(pf_ref.at[NX - 1, 1], sent))

    got(rf_ref, f3_recv)
    total = rf_ref[0, 0]
    for i in range(1, NX * 2):
        total += rf_ref[i // 2, i % 2]
    resp_ref[...] = total.astype(BF16)

    got(rb_ref, b3_recv)
    total = rb_ref[0]
    for i in range(1, NY):
        total += rb_ref[i]
    grad_ref[...] = total.astype(BF16)


def solution(mesh):
    ns = mesh.shape["sp"]

    def local(activations, weights, out_grad):
        act = activations.reshape(2 * B, LANES)
        grad = out_grad.reshape(B, -1)
        wide = grad.shape[1]
        w = jnp.swapaxes(weights, 3, 4).reshape(27, B, 2 * B)
        dma = pltpu.SemaphoreType.DMA
        responses, in_grad = pl.pallas_call(
            functools.partial(kernel, ns),
            out_shape=(
                pltpu.VMEM((B, wide), BF16),
                pltpu.VMEM((2 * B, LANES), BF16),
            ),
            in_specs=[pl.BlockSpec(memory_space=pl.ANY)] * 3,
            out_specs=(pl.BlockSpec(memory_space=pltpu.VMEM),) * 2,
            scratch_shapes=[
                pltpu.VMEM((2 * B, LANES), BF16),
                pltpu.VMEM((B, wide), BF16),
                pltpu.VMEM((27, B, 2 * B), BF16),
                pltpu.VMEM((NY, 3, 2 * B, LANES), BF16),
                pltpu.VMEM((2, 3, 2, 2 * B, wide), BF16),
                pltpu.VMEM((3, 2 * B, LANES), BF16),
                pltpu.VMEM((3, 2 * B, LANES), BF16),
                pltpu.VMEM((2, 3, 2, 9, B, LANES), BF16),
                pltpu.VMEM((192, 768), BF16),
                pltpu.VMEM((192, 768), BF16),
                pltpu.VMEM((768, NY * LANES), BF16),
                pltpu.VMEM((768, NY * LANES), BF16),
                pltpu.VMEM((NY, 2 * B, LANES), F32),
                pltpu.VMEM((NX, 2, B, wide), F32),
                pltpu.VMEM((NY, 2 * B, LANES), F32),
                pltpu.VMEM((NX, 2, B, wide), F32),
                dma((3,)), dma,
                dma((3,)), dma((3,)), dma((3,)), dma((2, 3)), dma((3,)), dma((6,)),
                dma, dma,
                pltpu.SemaphoreType.REGULAR,
            ],
            compiler_params=pltpu.CompilerParams(
                collective_id=0, has_side_effects=True, vmem_limit_bytes=60 * 1024 * 1024,
            ),
        )(act, w, grad)
        return responses.reshape(out_grad.shape), in_grad.reshape(activations.shape)

    return jax.shard_map(
        local,
        mesh=mesh,
        in_specs=(
            P("chan", "sp", "filt"),
            P(None, None, None, "chan", "filt"),
            P("filt", "sp", "chan"),
        ),
        out_specs=(P("filt", "sp", "chan"), P("chan", "sp", "filt")),
        check_vma=False,
    )
```

```python
import functools

import jax
import jax.numpy as jnp
from jax import lax
from jax.experimental import pallas as pl
from jax.experimental.pallas import tpu as pltpu
from jax.sharding import PartitionSpec as P

MESH = pl.DeviceIdType.MESH
BF16 = jnp.bfloat16
F32 = jnp.float32
B = 32
NX, NY = 4, 8
FAR = (4, 3, 5, 2, 6, 1, 7)
ORDER = (0, 1, 7, 2, 6, 3, 5, 4)
LANES = 128


def kernel(
    ns,
    act_hbm, w_hbm, og_hbm, resp_ref, grad_ref,
    a_ref, o_ref, w_ref, d_ref, g_ref, hd_ref, hg_ref, wr_ref, lf_ref, lb_ref, rg_ref, rd_ref,
    pb_ref, pf_ref, rb_ref, rf_ref,
    load_sem, sent, f1_recv, f2_recv, b1_recv, b2_recv, ws_recv, h_recv, b3_recv, f3_recv, up_sem,
):
    chan, filt, s = lax.axis_index("chan"), lax.axis_index("filt"), lax.axis_index("sp")
    x, core = chan // 2, chan % 2
    zl, y = filt // NY, filt % NY
    k, xi = x // 2, x % 2
    other = 1 - core
    has_low, has_high = s > 0, s < ns - 1
    relay = core == k
    stays = core == zl

    def dev(x_, core_, zl_, y_, s_):
        return (x_ * 2 + core_, zl_ * NY + y_, s_)

    def remote(src, dst, ssem, rsem, to):
        return pltpu.make_async_remote_copy(
            src_ref=src, dst_ref=dst, send_sem=ssem, recv_sem=rsem,
            device_id=to, device_id_type=MESH,
        )

    def got(ref, sem):
        pltpu.make_async_copy(ref, ref, sem).wait()

    def start(args, own=None):
        if own is None:
            remote(*args).start()
            return
        pl.when(jnp.logical_not(own))(lambda: remote(*args).start())
        pl.when(own)(lambda: pltpu.make_async_copy(args[0], args[1], args[3]).start())

    def finish(args, own=None):
        if own is None:
            remote(*args).wait_send()
        else:
            pl.when(jnp.logical_not(own))(lambda: remote(*args).wait_send())

    barrier = pltpu.get_barrier_semaphore()

    def greet(to, sem=barrier):
        pl.semaphore_signal(sem, inc=1, device_id=to, device_id_type=MESH)

    loads = [
        pltpu.make_async_copy(act_hbm, a_ref, load_sem.at[0]),
        pltpu.make_async_copy(og_hbm, o_ref, load_sem.at[1]),
        pltpu.make_async_copy(w_hbm, w_ref, load_sem.at[2]),
    ]
    for load in loads:
        load.start()
    for d in FAR:
        greet(dev(x, core, zl, (y + d) % NY, s))

    def greet_slab(ds):
        for dc in range(2):
            for dz in range(2):
                if (ds, dc, dz) != (0, 0, 0):
                    greet(dev(x, (core + dc) % 2, (zl + dz) % 2, y, s + ds))

    pl.when(has_high)(lambda: greet_slab(1))
    greet_slab(0)
    for d in range(1, NX):
        greet(dev((x + d) % NX, core, zl, y, s))

    def inside(p, body):
        if p == 1:
            body()
        else:
            pl.when(has_low if p == 0 else has_high)(body)

    def clear_planes(p):
        for r_ref in (rg_ref, rd_ref):
            r_ref[p * 256:(p + 1) * 256, :] = jnp.zeros((256, r_ref.shape[1]), BF16)

    pl.when(jnp.logical_not(has_low))(lambda: clear_planes(0))
    pl.when(jnp.logical_not(has_high))(lambda: clear_planes(2))
    loads[0].wait()
    loads[1].wait()
    count = (NY - 1) + 3 + (NX - 1)
    pl.semaphore_wait(barrier, count + 4 * has_low.astype(jnp.int32))

    @pl.when(has_low)
    def _():
        for dc in range(2):
            for dz in range(2):
                greet(dev(x, (core + dc) % 2, (zl + dz) % 2, y, s - 1), up_sem)

    def f1_sends(ds):
        for dz in range(2):
            z2 = (zl + dz) % 2
            start((a_ref.at[pl.ds(z2 * B, B), :], d_ref.at[y, 1 - ds, pl.ds(core * B, B), :],
                   sent, f1_recv.at[1 - ds], dev(x, zl, z2, y, s + ds)),
                  stays if (ds, dz) == (0, 0) else None)

    def f2_sends(p):
        for y2 in ORDER:
            @pl.when(y != y2)
            def _(y2=y2):
                start((d_ref.at[y, p], d_ref.at[y, p], sent, f2_recv.at[p], dev(x, core, zl, y2, s)))

    def b1_copy(ds, dz):
        z2 = (zl + dz) % 2
        return (
            o_ref,
            g_ref.at[xi, 1 - ds, core, pl.ds(zl * B, B), :],
            sent, b1_recv.at[1 - ds], dev(x, k, z2, y, s + ds),
        )

    def b1_sends(ds):
        for dz in range(2):
            start(b1_copy(ds, dz), relay if (ds, dz) == (0, 0) else None)

    pl.when(has_low)(lambda: f1_sends(-1))
    pl.when(has_low)(lambda: b1_sends(-1))
    f1_sends(0)
    b1_sends(0)

    loads[2].wait()
    blank = jnp.zeros((B, B), BF16)
    for h in range(2):
        slot = jnp.where(zl == h, h, 2)
        for a in range(3):
            for e in range(3):
                taps = [w_ref[a * 9 + b * 3 + e] for b in range(3)]
                wr_ref[core, slot, 0, a * 3 + e] = jnp.concatenate(
                    [t[:, h * B:(h + 1) * B] for t in taps] + [blank], axis=1)
    w_across = (wr_ref.at[core, 2, 0], wr_ref.at[core, zl, 0], sent, ws_recv.at[0], dev(x, core, 1 - zl, y, s))
    w_own = (wr_ref.at[core, zl], wr_ref.at[core, zl], sent, ws_recv.at[1], dev(x, other, zl, y, s))
    w_next = (wr_ref.at[core, 1 - zl], wr_ref.at[core, 1 - zl], sent, ws_recv.at[2], dev(x, other, zl, y, s))
    start(w_across)
    got(d_ref.at[y, 1], f1_recv.at[1])
    f2_sends(1)

    def turn(slot):
        for i in range(9):
            flip = wr_ref[core, slot, 0, i].astype(F32).T
            wr_ref[core, slot, 1, i] = jnp.concatenate(
                [flip[(2 - b) * B:(3 - b) * B] for b in range(3)] + [flip[3 * B:]], axis=1).astype(BF16)

    @pl.when(has_high)
    def _():
        pl.semaphore_wait(up_sem, 4)
        b1_sends(1)
        f1_sends(1)

    def b2_copy(p, d):
        return (g_ref.at[xi, p], g_ref.at[xi, p], sent, b2_recv.at[xi, p],
                dev((x + d) % NX, core, zl, y, s))

    def b2_sends(p):
        for d in (2, 1, 3):
            start(b2_copy(p, d))

    @pl.when(relay)
    def _():
        got(g_ref.at[xi, 1], b1_recv.at[1])
        b2_sends(1)

    @pl.when(has_low)
    def _():
        got(d_ref.at[y, 0], f1_recv.at[0])
        f2_sends(0)

    @pl.when(has_high)
    def _():
        got(d_ref.at[y, 2], f1_recv.at[2])
        f2_sends(2)

    for p, has in ((0, has_low), (2, has_high)):
        @pl.when(jnp.logical_and(relay, has))
        def _(p=p):
            got(g_ref.at[xi, p], b1_recv.at[p])
            b2_sends(p)

    turn(zl)
    start(w_own)
    got(wr_ref.at[core, 1 - zl, 0], ws_recv.at[0])
    turn(1 - zl)
    start(w_next)

    def low_g(p):
        return (g_ref.at[0, p, 0, :, pl.ds(0, LANES)], hg_ref.at[p], sent, h_recv.at[p], dev(x, other, zl, y, s))

    def high_g(p):
        return (g_ref.at[1, p, 1, :, pl.ds(LANES, LANES)], hg_ref.at[p], sent, h_recv.at[p], dev(x, other, zl, y, s))

    def low_d(p):
        return (d_ref.at[0, p], hd_ref.at[p], sent, h_recv.at[3 + p], dev(x, other, zl, y, s))

    def high_d(p):
        return (d_ref.at[NY - 1, p], hd_ref.at[p], sent, h_recv.at[3 + p], dev(x, other, zl, y, s))

    remote(*w_own).wait_recv()
    remote(*w_next).wait_recv()
    for cs in range(2):
        for z in range(2):
            for a in range(3):
                for e in range(3):
                    lf_ref[e * 64 + z * B:e * 64 + z * B + B, a * 256 + cs * 128:a * 256 + cs * 128 + 128] = (
                        wr_ref[cs, z, 0, a * 3 + e])
                    lb_ref[e * 64 + cs * B:e * 64 + cs * B + B, a * 256 + z * 128:a * 256 + z * 128 + 128] = (
                        wr_ref[cs, z, 1, (2 - a) * 3 + 2 - e])

    lane = lax.broadcasted_iota(jnp.int32, (64, LANES), 1)
    left_half = lane < 64
    inside_low = lane % 64 != 0
    inside_high = lane % 64 != 63

    def put(r_ref, a, b, t, tile):
        for c in range(2):
            row = a * 256 + c * 128 + b * B
            r_ref[row:row + B, t * LANES:(t + 1) * LANES] = tile[c * B:(c + 1) * B]

    def half_turn(tile):
        return pltpu.roll(tile.astype(F32), 64, axis=1)

    def rows(r_ref, a, tile_of):
        for c in range(2):
            row = a * 256 + c * 128 + 3 * B
            r_ref[row:row + B, :] = jnp.zeros((B, r_ref.shape[1]), BF16)
        turned = None
        for t in range(NY):
            tile = tile_of(a, t)
            put(r_ref, a, 1, t, tile)
            before, turned = turned, half_turn(tile)
            if t > 0:
                mid = jnp.where(left_half, before, turned).astype(BF16)
                put(r_ref, a, 0, t, mid)
                put(r_ref, a, 2, t - 1, mid)

    def edge_rows(r_ref, a, tile_of, halo):
        turned = half_turn(halo)
        none = jnp.zeros_like(turned)
        low = jnp.where(core == 1, turned, none)
        high = jnp.where(core == 0, turned, none)
        put(r_ref, a, 0, 0, jnp.where(left_half, low, half_turn(tile_of(a, 0))).astype(BF16))
        put(r_ref, a, 2, NY - 1, jnp.where(left_half, half_turn(tile_of(a, NY - 1)), high).astype(BF16))

    def multiply(l_ref, r_ref, pair, emit):
        part = jnp.dot(l_ref[...], r_ref[:, pair * 256:(pair + 1) * 256], preferred_element_type=F32)
        for h in range(2):
            piece = part[:, h * LANES:(h + 1) * LANES]
            total = piece[64:128]
            total += jnp.where(inside_low, pltpu.roll(piece[0:64], 1, axis=1), 0.0)
            total += jnp.where(inside_high, pltpu.roll(piece[128:192], LANES - 1, axis=1), 0.0)
            emit(pair * 2 + h, total)

    def g_tile(a, t):
        return g_ref[t // 4, a, t // 2 % 2, :, t % 2 * LANES:(t % 2 + 1) * LANES]

    def emit_b(t, total):
        pb_ref[t] = total

    def b3_sends(tiles):
        for t in tiles:
            for dc in range(2):
                c2 = (core + dc) % 2
                start((pb_ref.at[t, pl.ds(c2 * B, B), :], rb_ref.at[y, pl.ds(zl * B, B), :],
                       sent, b3_recv, dev(x, c2, core, t, s)),
                      jnp.logical_and(stays, y == t) if dc == 0 else None)

    def g_plane(p):
        for i in range(2):
            pl.when(jnp.logical_not(jnp.logical_and(relay, xi == i)))(
                lambda i=i: got(g_ref.at[i, p], b2_recv.at[i, p]))
        pl.when(core == 0)(lambda: start(high_g(p)))
        pl.when(core == 1)(lambda: start(low_g(p)))
        rows(rg_ref, p, g_tile)

    def g_edges(p):
        got(hg_ref.at[p], h_recv.at[p])
        edge_rows(rg_ref, p, g_tile, hg_ref[p])

    for p in (1, 0, 2):
        inside(p, functools.partial(g_plane, p))
    multiply(lb_ref, rg_ref, 1, emit_b)
    got(d_ref.at[pl.ds(0, NY - 1), 1], f2_recv.at[1])
    b3_sends((2, 3))
    for p in range(3):
        inside(p, functools.partial(g_edges, p))
    for pair in (0, 3, 2):
        multiply(lb_ref, rg_ref, pair, emit_b)
        b3_sends((2 * pair, 2 * pair + 1))

    def d_tile(a, t):
        return d_ref[t, a]

    def d_plane(p):
        if p != 1:
            got(d_ref.at[pl.ds(0, NY - 1), p], f2_recv.at[p])
        pl.when(core == 0)(lambda: start(high_d(p)))
        pl.when(core == 1)(lambda: start(low_d(p)))
        rows(rd_ref, p, d_tile)

    def d_edges(p):
        got(hd_ref.at[p], h_recv.at[3 + p])
        edge_rows(rd_ref, p, d_tile, hd_ref[p])

    for p in (1, 0, 2):
        inside(p, functools.partial(d_plane, p))

    def emit_f(t, total):
        for z in range(2):
            pf_ref[t // 2, z, :, t % 2 * LANES:(t % 2 + 1) * LANES] = total[z * B:(z + 1) * B]

    def f3_sends(j):
        for dz in range(2):
            x2, c2, z2 = core * 2 + j // 2, j % 2, (zl + dz) % 2
            own = jnp.logical_and(x2 == x, c2 == core) if dz == 0 else None
            start((pf_ref.at[j, z2], rf_ref.at[x, zl], sent, f3_recv, dev(x2, c2, z2, y, s)), own)

    for pair in (1,):
        multiply(lf_ref, rd_ref, pair, emit_f)
        f3_sends(pair)
    for p in range(3):
        inside(p, functools.partial(d_edges, p))
    for pair in (0, 2, 3):
        multiply(lf_ref, rd_ref, pair, emit_f)
        f3_sends(pair)

    pl.when(has_low)(lambda: got(a_ref, sent))
    pl.when(has_high)(lambda: got(a_ref, sent))
    got(a_ref.at[pl.ds(0, B)], sent)
    pl.when(jnp.logical_not(stays))(lambda: got(a_ref.at[pl.ds(B, B)], sent))
    pair = g_ref.at[0, 0, 0]
    pl.when(has_low)(lambda: got(pair, sent))
    pl.when(has_high)(lambda: got(pair, sent))
    pl.when(relay)(lambda: got(pair.at[pl.ds(0, B)], sent))
    pl.when(jnp.logical_not(relay))(lambda: got(pair, sent))
    got(d_ref.at[pl.ds(0, NY - 1), 1], sent)
    pl.when(has_low)(lambda: got(d_ref.at[pl.ds(0, NY - 1), 0], sent))
    pl.when(has_high)(lambda: got(d_ref.at[pl.ds(0, NY - 1), 2], sent))
    for copy in (w_across, w_own, w_next):
        finish(copy)

    @pl.when(relay)
    def _():
        for p in range(3):
            inside(p, lambda: got(g_ref.at[0], sent))

    for p in range(3):
        inside(p, lambda p=p: got(hg_ref.at[p], sent))
        inside(p, lambda p=p: got(hd_ref.at[p], sent))
    got(pb_ref.at[pl.ds(0, NY - 1)], sent)
    got(pb_ref.at[NY - 1, pl.ds(0, B)], sent)
    pl.when(jnp.logical_not(stays))(lambda: got(pb_ref.at[NY - 1, pl.ds(B, B)], sent))
    got(pf_ref.at[pl.ds(0, NX - 1)], sent)
    got(pf_ref.at[NX - 1, 0], sent)
    pl.when(jnp.logical_not(relay))(lambda: got(pf_ref.at[NX - 1, 1], sent))

    got(rf_ref, f3_recv)
    total = rf_ref[0, 0]
    for i in range(1, NX * 2):
        total += rf_ref[i // 2, i % 2]
    resp_ref[...] = total.astype(BF16)

    got(rb_ref, b3_recv)
    total = rb_ref[0]
    for i in range(1, NY):
        total += rb_ref[i]
    grad_ref[...] = total.astype(BF16)


def solution(mesh):
    ns = mesh.shape["sp"]

    def local(activations, weights, out_grad):
        act = activations.reshape(2 * B, LANES)
        grad = out_grad.reshape(B, -1)
        wide = grad.shape[1]
        w = jnp.swapaxes(weights, 3, 4).reshape(27, B, 2 * B)
        dma = pltpu.SemaphoreType.DMA
        responses, in_grad = pl.pallas_call(
            functools.partial(kernel, ns),
            out_shape=(
                pltpu.VMEM((B, wide), BF16),
                pltpu.VMEM((2 * B, LANES), BF16),
            ),
            in_specs=[pl.BlockSpec(memory_space=pl.ANY)] * 3,
            out_specs=(pl.BlockSpec(memory_space=pltpu.VMEM),) * 2,
            scratch_shapes=[
                pltpu.VMEM((2 * B, LANES), BF16),
                pltpu.VMEM((B, wide), BF16),
                pltpu.VMEM((27, B, 2 * B), BF16),
                pltpu.VMEM((NY, 3, 2 * B, LANES), BF16),
                pltpu.VMEM((2, 3, 2, 2 * B, wide), BF16),
                pltpu.VMEM((3, 2 * B, LANES), BF16),
                pltpu.VMEM((3, 2 * B, LANES), BF16),
                pltpu.VMEM((2, 3, 2, 9, B, LANES), BF16),
                pltpu.VMEM((192, 768), BF16),
                pltpu.VMEM((192, 768), BF16),
                pltpu.VMEM((768, NY * LANES), BF16),
                pltpu.VMEM((768, NY * LANES), BF16),
                pltpu.VMEM((NY, 2 * B, LANES), F32),
                pltpu.VMEM((NX, 2, B, wide), F32),
                pltpu.VMEM((NY, 2 * B, LANES), F32),
                pltpu.VMEM((NX, 2, B, wide), F32),
                dma((3,)), dma,
                dma((3,)), dma((3,)), dma((3,)), dma((2, 3)), dma((3,)), dma((6,)),
                dma, dma,
                pltpu.SemaphoreType.REGULAR,
            ],
            compiler_params=pltpu.CompilerParams(
                collective_id=0, has_side_effects=True, vmem_limit_bytes=60 * 1024 * 1024,
            ),
        )(act, w, grad)
        return responses.reshape(out_grad.shape), in_grad.reshape(activations.shape)

    return jax.shard_map(
        local,
        mesh=mesh,
        in_specs=(
            P("chan", "sp", "filt"),
            P(None, None, None, "chan", "filt"),
            P("filt", "sp", "chan"),
        ),
        out_specs=(P("filt", "sp", "chan"), P("chan", "sp", "filt")),
        check_vma=False,
    )
```

```python
import functools

import jax
import jax.numpy as jnp
from jax import lax
from jax.experimental import pallas as pl
from jax.experimental.pallas import tpu as pltpu
from jax.sharding import PartitionSpec as P

MESH = pl.DeviceIdType.MESH
BF16 = jnp.bfloat16
F32 = jnp.float32
B = 32
NX, NY = 4, 8
FAR = (4, 3, 5, 2, 6, 1, 7)
ORDER = (0, 1, 7, 2, 6, 3, 5, 4)
LANES = 128


def kernel(
    ns,
    act_hbm, w_hbm, og_hbm, resp_ref, grad_ref,
    a_ref, o_ref, w_ref, d_ref, g_ref, hd_ref, hg_ref, wr_ref, lf_ref, lb_ref, rg_ref, rd_ref,
    pb_ref, pf_ref, rb_ref, rf_ref,
    load_sem, sent, f1_recv, f2_recv, b1_recv, b2_recv, ws_recv, h_recv, b3_recv, f3_recv, up_sem,
):
    chan, filt, s = lax.axis_index("chan"), lax.axis_index("filt"), lax.axis_index("sp")
    x, core = chan // 2, chan % 2
    zl, y = filt // NY, filt % NY
    k, xi = x // 2, x % 2
    other = 1 - core
    has_low, has_high = s > 0, s < ns - 1
    relay = core == k
    stays = core == zl

    def dev(x_, core_, zl_, y_, s_):
        return (x_ * 2 + core_, zl_ * NY + y_, s_)

    def remote(src, dst, ssem, rsem, to):
        return pltpu.make_async_remote_copy(
            src_ref=src, dst_ref=dst, send_sem=ssem, recv_sem=rsem,
            device_id=to, device_id_type=MESH,
        )

    def got(ref, sem):
        pltpu.make_async_copy(ref, ref, sem).wait()

    def start(args, own=None):
        if own is None:
            remote(*args).start()
            return
        pl.when(jnp.logical_not(own))(lambda: remote(*args).start())
        pl.when(own)(lambda: pltpu.make_async_copy(args[0], args[1], args[3]).start())

    def finish(args, own=None):
        if own is None:
            remote(*args).wait_send()
        else:
            pl.when(jnp.logical_not(own))(lambda: remote(*args).wait_send())

    barrier = pltpu.get_barrier_semaphore()

    def greet(to, sem=barrier):
        pl.semaphore_signal(sem, inc=1, device_id=to, device_id_type=MESH)

    loads = [
        pltpu.make_async_copy(act_hbm, a_ref, load_sem.at[0]),
        pltpu.make_async_copy(og_hbm, o_ref, load_sem.at[1]),
        pltpu.make_async_copy(w_hbm, w_ref, load_sem.at[2]),
    ]
    for load in loads:
        load.start()
    for d in FAR:
        greet(dev(x, core, zl, (y + d) % NY, s))

    def greet_slab(ds):
        for dc in range(2):
            for dz in range(2):
                if (ds, dc, dz) != (0, 0, 0):
                    greet(dev(x, (core + dc) % 2, (zl + dz) % 2, y, s + ds))

    pl.when(has_high)(lambda: greet_slab(1))
    greet_slab(0)
    for d in range(1, NX):
        greet(dev((x + d) % NX, core, zl, y, s))

    def inside(p, body):
        if p == 1:
            body()
        else:
            pl.when(has_low if p == 0 else has_high)(body)

    def clear_planes(p):
        for r_ref in (rg_ref, rd_ref):
            r_ref[p * 256:(p + 1) * 256, :] = jnp.zeros((256, r_ref.shape[1]), BF16)

    pl.when(jnp.logical_not(has_low))(lambda: clear_planes(0))
    pl.when(jnp.logical_not(has_high))(lambda: clear_planes(2))
    loads[0].wait()
    loads[1].wait()
    count = (NY - 1) + 3 + (NX - 1)
    pl.semaphore_wait(barrier, count + 4 * has_low.astype(jnp.int32))

    @pl.when(has_low)
    def _():
        for dc in range(2):
            for dz in range(2):
                greet(dev(x, (core + dc) % 2, (zl + dz) % 2, y, s - 1), up_sem)

    def f1_sends(ds):
        for dz in range(2):
            z2 = (zl + dz) % 2
            start((a_ref.at[pl.ds(z2 * B, B), :], d_ref.at[y, 1 - ds, pl.ds(core * B, B), :],
                   sent, f1_recv.at[1 - ds], dev(x, zl, z2, y, s + ds)),
                  stays if (ds, dz) == (0, 0) else None)

    def f2_sends(p):
        for y2 in ORDER:
            @pl.when(y != y2)
            def _(y2=y2):
                start((d_ref.at[y, p], d_ref.at[y, p], sent, f2_recv.at[p], dev(x, core, zl, y2, s)))

    def b1_copy(ds, dz):
        z2 = (zl + dz) % 2
        return (
            o_ref,
            g_ref.at[xi, 1 - ds, core, pl.ds(zl * B, B), :],
            sent, b1_recv.at[1 - ds], dev(x, k, z2, y, s + ds),
        )

    def b1_sends(ds):
        for dz in range(2):
            start(b1_copy(ds, dz), relay if (ds, dz) == (0, 0) else None)

    pl.when(has_low)(lambda: f1_sends(-1))
    pl.when(has_low)(lambda: b1_sends(-1))
    f1_sends(0)
    b1_sends(0)

    loads[2].wait()
    blank = jnp.zeros((B, B), BF16)
    for h in range(2):
        slot = jnp.where(zl == h, h, 2)
        for a in range(3):
            for e in range(3):
                taps = [w_ref[a * 9 + b * 3 + e] for b in range(3)]
                wr_ref[core, slot, 0, a * 3 + e] = jnp.concatenate(
                    [t[:, h * B:(h + 1) * B] for t in taps] + [blank], axis=1)
    w_across = (wr_ref.at[core, 2, 0], wr_ref.at[core, zl, 0], sent, ws_recv.at[0], dev(x, core, 1 - zl, y, s))
    w_own = (wr_ref.at[core, zl], wr_ref.at[core, zl], sent, ws_recv.at[1], dev(x, other, zl, y, s))
    w_next = (wr_ref.at[core, 1 - zl], wr_ref.at[core, 1 - zl], sent, ws_recv.at[2], dev(x, other, zl, y, s))
    start(w_across)
    got(d_ref.at[y, 1], f1_recv.at[1])
    f2_sends(1)

    def turn(slot):
        for i in range(9):
            flip = wr_ref[core, slot, 0, i].astype(F32).T
            wr_ref[core, slot, 1, i] = jnp.concatenate(
                [flip[(2 - b) * B:(3 - b) * B] for b in range(3)] + [flip[3 * B:]], axis=1).astype(BF16)

    @pl.when(has_high)
    def _():
        pl.semaphore_wait(up_sem, 4)
        b1_sends(1)
        f1_sends(1)

    def b2_copy(p, d):
        return (g_ref.at[xi, p], g_ref.at[xi, p], sent, b2_recv.at[xi, p],
                dev((x + d) % NX, core, zl, y, s))

    def b2_sends(p):
        for d in (2, 1, 3):
            start(b2_copy(p, d))

    @pl.when(relay)
    def _():
        got(g_ref.at[xi, 1], b1_recv.at[1])
        b2_sends(1)

    @pl.when(has_low)
    def _():
        got(d_ref.at[y, 0], f1_recv.at[0])
        f2_sends(0)

    @pl.when(has_high)
    def _():
        got(d_ref.at[y, 2], f1_recv.at[2])
        f2_sends(2)

    for p, has in ((0, has_low), (2, has_high)):
        @pl.when(jnp.logical_and(relay, has))
        def _(p=p):
            got(g_ref.at[xi, p], b1_recv.at[p])
            b2_sends(p)

    turn(zl)
    start(w_own)
    got(wr_ref.at[core, 1 - zl, 0], ws_recv.at[0])
    turn(1 - zl)
    start(w_next)

    def low_g(p):
        return (g_ref.at[0, p, 0, :, pl.ds(0, LANES)], hg_ref.at[p], sent, h_recv.at[p], dev(x, other, zl, y, s))

    def high_g(p):
        return (g_ref.at[1, p, 1, :, pl.ds(LANES, LANES)], hg_ref.at[p], sent, h_recv.at[p], dev(x, other, zl, y, s))

    def low_d(p):
        return (d_ref.at[0, p], hd_ref.at[p], sent, h_recv.at[3 + p], dev(x, other, zl, y, s))

    def high_d(p):
        return (d_ref.at[NY - 1, p], hd_ref.at[p], sent, h_recv.at[3 + p], dev(x, other, zl, y, s))

    remote(*w_own).wait_recv()
    remote(*w_next).wait_recv()
    for cs in range(2):
        for z in range(2):
            for a in range(3):
                for e in range(3):
                    lf_ref[e * 64 + z * B:e * 64 + z * B + B, a * 256 + cs * 128:a * 256 + cs * 128 + 128] = (
                        wr_ref[cs, z, 0, a * 3 + e])
                    lb_ref[e * 64 + cs * B:e * 64 + cs * B + B, a * 256 + z * 128:a * 256 + z * 128 + 128] = (
                        wr_ref[cs, z, 1, (2 - a) * 3 + 2 - e])

    lane = lax.broadcasted_iota(jnp.int32, (64, LANES), 1)
    left_half = lane < 64
    inside_low = lane % 64 != 0
    inside_high = lane % 64 != 63

    def put(r_ref, a, b, t, tile):
        for c in range(2):
            row = a * 256 + c * 128 + b * B
            r_ref[row:row + B, t * LANES:(t + 1) * LANES] = tile[c * B:(c + 1) * B]

    def half_turn(tile):
        return pltpu.roll(tile.astype(F32), 64, axis=1)

    def rows(r_ref, a, tile_of):
        for c in range(2):
            row = a * 256 + c * 128 + 3 * B
            r_ref[row:row + B, :] = jnp.zeros((B, r_ref.shape[1]), BF16)
        turned = None
        for t in range(NY):
            tile = tile_of(a, t)
            put(r_ref, a, 1, t, tile)
            before, turned = turned, half_turn(tile)
            if t > 0:
                mid = jnp.where(left_half, before, turned).astype(BF16)
                put(r_ref, a, 0, t, mid)
                put(r_ref, a, 2, t - 1, mid)

    def edge_rows(r_ref, a, tile_of, halo):
        turned = half_turn(halo)
        none = jnp.zeros_like(turned)
        low = jnp.where(core == 1, turned, none)
        high = jnp.where(core == 0, turned, none)
        put(r_ref, a, 0, 0, jnp.where(left_half, low, half_turn(tile_of(a, 0))).astype(BF16))
        put(r_ref, a, 2, NY - 1, jnp.where(left_half, half_turn(tile_of(a, NY - 1)), high).astype(BF16))

    def multiply(l_ref, r_ref, pair, emit):
        part = jnp.dot(l_ref[...], r_ref[:, pair * 256:(pair + 1) * 256], preferred_element_type=F32)
        for h in range(2):
            piece = part[:, h * LANES:(h + 1) * LANES]
            total = piece[64:128]
            total += jnp.where(inside_low, pltpu.roll(piece[0:64], 1, axis=1), 0.0)
            total += jnp.where(inside_high, pltpu.roll(piece[128:192], LANES - 1, axis=1), 0.0)
            emit(pair * 2 + h, total)

    def g_tile(a, t):
        return g_ref[t // 4, a, t // 2 % 2, :, t % 2 * LANES:(t % 2 + 1) * LANES]

    def emit_b(t, total):
        pb_ref[t] = total

    def b3_sends(tiles):
        for t in tiles:
            for dc in range(2):
                c2 = (core + dc) % 2
                start((pb_ref.at[t, pl.ds(c2 * B, B), :], rb_ref.at[y, pl.ds(zl * B, B), :],
                       sent, b3_recv, dev(x, c2, core, t, s)),
                      jnp.logical_and(stays, y == t) if dc == 0 else None)

    def g_plane(p):
        for i in range(2):
            pl.when(jnp.logical_not(jnp.logical_and(relay, xi == i)))(
                lambda i=i: got(g_ref.at[i, p], b2_recv.at[i, p]))
        pl.when(core == 0)(lambda: start(high_g(p)))
        pl.when(core == 1)(lambda: start(low_g(p)))
        rows(rg_ref, p, g_tile)

    def g_edges(p):
        got(hg_ref.at[p], h_recv.at[p])
        edge_rows(rg_ref, p, g_tile, hg_ref[p])

    for p in (1, 2, 0):
        inside(p, functools.partial(g_plane, p))
    multiply(lb_ref, rg_ref, 1, emit_b)
    got(d_ref.at[pl.ds(0, NY - 1), 1], f2_recv.at[1])
    b3_sends((2, 3))
    for p in range(3):
        inside(p, functools.partial(g_edges, p))
    for pair in (0, 3, 2):
        multiply(lb_ref, rg_ref, pair, emit_b)
        b3_sends((2 * pair, 2 * pair + 1))

    def d_tile(a, t):
        return d_ref[t, a]

    def d_plane(p):
        if p != 1:
            got(d_ref.at[pl.ds(0, NY - 1), p], f2_recv.at[p])
        pl.when(core == 0)(lambda: start(high_d(p)))
        pl.when(core == 1)(lambda: start(low_d(p)))
        rows(rd_ref, p, d_tile)

    def d_edges(p):
        got(hd_ref.at[p], h_recv.at[3 + p])
        edge_rows(rd_ref, p, d_tile, hd_ref[p])

    for p in (1, 2, 0):
        inside(p, functools.partial(d_plane, p))

    def emit_f(t, total):
        for z in range(2):
            pf_ref[t // 2, z, :, t % 2 * LANES:(t % 2 + 1) * LANES] = total[z * B:(z + 1) * B]

    def f3_sends(j):
        for dz in range(2):
            x2, c2, z2 = core * 2 + j // 2, j % 2, (zl + dz) % 2
            own = jnp.logical_and(x2 == x, c2 == core) if dz == 0 else None
            start((pf_ref.at[j, z2], rf_ref.at[x, zl], sent, f3_recv, dev(x2, c2, z2, y, s)), own)

    for pair in (1,):
        multiply(lf_ref, rd_ref, pair, emit_f)
        f3_sends(pair)
    for p in range(3):
        inside(p, functools.partial(d_edges, p))
    for pair in (0, 2, 3):
        multiply(lf_ref, rd_ref, pair, emit_f)
        f3_sends(pair)

    pl.when(has_low)(lambda: got(a_ref, sent))
    pl.when(has_high)(lambda: got(a_ref, sent))
    got(a_ref.at[pl.ds(0, B)], sent)
    pl.when(jnp.logical_not(stays))(lambda: got(a_ref.at[pl.ds(B, B)], sent))
    pair = g_ref.at[0, 0, 0]
    pl.when(has_low)(lambda: got(pair, sent))
    pl.when(has_high)(lambda: got(pair, sent))
    pl.when(relay)(lambda: got(pair.at[pl.ds(0, B)], sent))
    pl.when(jnp.logical_not(relay))(lambda: got(pair, sent))
    got(d_ref.at[pl.ds(0, NY - 1), 1], sent)
    pl.when(has_low)(lambda: got(d_ref.at[pl.ds(0, NY - 1), 0], sent))
    pl.when(has_high)(lambda: got(d_ref.at[pl.ds(0, NY - 1), 2], sent))
    for copy in (w_across, w_own, w_next):
        finish(copy)

    @pl.when(relay)
    def _():
        for p in range(3):
            inside(p, lambda: got(g_ref.at[0], sent))

    for p in range(3):
        inside(p, lambda p=p: got(hg_ref.at[p], sent))
        inside(p, lambda p=p: got(hd_ref.at[p], sent))
    got(pb_ref.at[pl.ds(0, NY - 1)], sent)
    got(pb_ref.at[NY - 1, pl.ds(0, B)], sent)
    pl.when(jnp.logical_not(stays))(lambda: got(pb_ref.at[NY - 1, pl.ds(B, B)], sent))
    got(pf_ref.at[pl.ds(0, NX - 1)], sent)
    got(pf_ref.at[NX - 1, 0], sent)
    pl.when(jnp.logical_not(relay))(lambda: got(pf_ref.at[NX - 1, 1], sent))

    got(rf_ref, f3_recv)
    total = rf_ref[0, 0]
    for i in range(1, NX * 2):
        total += rf_ref[i // 2, i % 2]
    resp_ref[...] = total.astype(BF16)

    got(rb_ref, b3_recv)
    total = rb_ref[0]
    for i in range(1, NY):
        total += rb_ref[i]
    grad_ref[...] = total.astype(BF16)


def solution(mesh):
    ns = mesh.shape["sp"]

    def local(activations, weights, out_grad):
        act = activations.reshape(2 * B, LANES)
        grad = out_grad.reshape(B, -1)
        wide = grad.shape[1]
        w = jnp.swapaxes(weights, 3, 4).reshape(27, B, 2 * B)
        dma = pltpu.SemaphoreType.DMA
        responses, in_grad = pl.pallas_call(
            functools.partial(kernel, ns),
            out_shape=(
                pltpu.VMEM((B, wide), BF16),
                pltpu.VMEM((2 * B, LANES), BF16),
            ),
            in_specs=[pl.BlockSpec(memory_space=pl.ANY)] * 3,
            out_specs=(pl.BlockSpec(memory_space=pltpu.VMEM),) * 2,
            scratch_shapes=[
                pltpu.VMEM((2 * B, LANES), BF16),
                pltpu.VMEM((B, wide), BF16),
                pltpu.VMEM((27, B, 2 * B), BF16),
                pltpu.VMEM((NY, 3, 2 * B, LANES), BF16),
                pltpu.VMEM((2, 3, 2, 2 * B, wide), BF16),
                pltpu.VMEM((3, 2 * B, LANES), BF16),
                pltpu.VMEM((3, 2 * B, LANES), BF16),
                pltpu.VMEM((2, 3, 2, 9, B, LANES), BF16),
                pltpu.VMEM((192, 768), BF16),
                pltpu.VMEM((192, 768), BF16),
                pltpu.VMEM((768, NY * LANES), BF16),
                pltpu.VMEM((768, NY * LANES), BF16),
                pltpu.VMEM((NY, 2 * B, LANES), F32),
                pltpu.VMEM((NX, 2, B, wide), F32),
                pltpu.VMEM((NY, 2 * B, LANES), F32),
                pltpu.VMEM((NX, 2, B, wide), F32),
                dma((3,)), dma,
                dma((3,)), dma((3,)), dma((3,)), dma((2, 3)), dma((3,)), dma((6,)),
                dma, dma,
                pltpu.SemaphoreType.REGULAR,
            ],
            compiler_params=pltpu.CompilerParams(
                collective_id=0, has_side_effects=True, vmem_limit_bytes=60 * 1024 * 1024,
            ),
        )(act, w, grad)
        return responses.reshape(out_grad.shape), in_grad.reshape(activations.shape)

    return jax.shard_map(
        local,
        mesh=mesh,
        in_specs=(
            P("chan", "sp", "filt"),
            P(None, None, None, "chan", "filt"),
            P("filt", "sp", "chan"),
        ),
        out_specs=(P("filt", "sp", "chan"), P("chan", "sp", "filt")),
        check_vma=False,
    )
```
